256 devices in a mesh: acq: 64 (over z, y, core), strip: 4 (over x).
Axes of the slice: x: 4, y: 4, z: 8, core: 2. Of those that a mesh axis runs over, the one named last changes fastest.
Arguments:
- slc_stack: bfloat16 [256, 2, 4, 64, 2048], P('acq', None, 'strip')
- date_pairs: int32 [1024, 2], replicated, may hold values from 0 to 255, as said below
- pair_owner: int32 [1024, 1], replicated, may hold values from 0 to 63; in each aligned block of 1024 rows (0 to 1023, 1024 to 2047, ...) at most 32 rows name the same one
- pseudo_inverse: float32 [256, 1024], replicated, may hold values from -0.1875 to 0.1875
Outputs:
- series_parts: float32 [4, 64, 2, 32, 256], P('strip', 'acq')
- coherence_slots: float32 [2048, 2, 4, 2048], P('acq', None, 'strip')
The draws below stay inside these ranges and needn't reach their ends.
Inputs may be any that keep to these rules, and one draw needn't show every extreme that they name: `date_pairs`: each pair names two acquisitions, the second later than the first by 1 to 8. `pair_owner`: no owner stores more than 32 pairs; some owner stores exactly 32; every owner stores some.
All inputs are finite; a program needn't handle non-finite values.
Results may differ from the reference program's by a relative error of at most 0.0003.
Values may be sent and summed in bfloat16 or wider, within the bound.
No kernel may reach another device: no remote copies, remote signals or barrier semaphores. Data moves between devices by JAX's collectives and lax.ppermute only.
A program may use at most 128 MiB of HBM per device.

```python
import math
import jax
import jax.numpy as jnp
import numpy as np
from jax import lax

ROWS_DEV = 64
COL_DEV = 32
SPAN = 8
ACQS = 256
PAIRS = 1024
CAP = 32
NR = 256
COLS = 2048
N_ACQ = 64
N_STRIP = 4


def draw_slc_stack(key, part):
    key = jax.random.fold_in(key, 11)
    keys = jax.random.split(key, 6)
    base_real = jax.random.normal(keys[0], (NR, COLS), jnp.float32)
    base_imag = jax.random.normal(keys[1], (NR, COLS), jnp.float32)
    rough = jax.random.normal(keys[2], (NR, COLS), jnp.float32)
    rows_frac = jnp.arange(NR, dtype=jnp.float32)[:, None] / NR
    cols_frac = jnp.arange(COLS, dtype=jnp.float32)[None, :] / COLS
    surface = rough + 2.0 * rows_frac + 1.5 * cols_frac
    timing = jax.random.uniform(keys[3], (ACQS,), jnp.float32, -1.0, 1.0)
    amplitude = jnp.exp(jax.random.uniform(keys[4], (ACQS,), jnp.float32, -0.7, 0.7))
    noise = 0.7 * jax.random.normal(keys[5], (ACQS, 2, NR, COLS), jnp.float32)
    row_scale = jnp.ones((NR, 1), jnp.float32)
    phase = 1.2 * timing[:, None, None] * surface[None]
    cosine = jnp.cos(phase)
    sine = jnp.sin(phase)
    lead = amplitude[:, None, None] * row_scale[None]
    real_part = lead * (base_real[None] * cosine - base_imag[None] * sine) + noise[:, 0]
    imag_part = lead * (base_real[None] * sine + base_imag[None] * cosine) + noise[:, 1]
    image = jnp.stack([real_part, imag_part], axis=1)
    tiled = image.reshape(ACQS, 2, N_STRIP, ROWS_DEV, N_ACQ, COL_DEV).transpose(0, 1, 2, 4, 3, 5)
    return tiled.reshape(ACQS, 2, N_STRIP, N_ACQ, ROWS_DEV * COL_DEV).astype(jnp.bfloat16)


def draw_date_pairs(key, part):
    key = jax.random.fold_in(key, 23)
    keys = jax.random.split(key, 3)
    first_try = jax.random.randint(keys[0], (PAIRS,), 0, ACQS - SPAN)
    second_try = jax.random.randint(keys[1], (PAIRS,), 0, ACQS - SPAN)
    earlier = jnp.minimum(first_try, second_try)
    later = earlier + jax.random.randint(keys[2], (PAIRS,), 1, SPAN + 1)
    earlier = earlier.at[PAIRS - 1].set(ACQS - 1 - SPAN).at[0].set(0)
    later = later.at[PAIRS - 1].set(ACQS - 1).at[0].set(1)
    return jnp.stack([earlier, later], axis=1).astype(jnp.int32)


def assign_block(key, own, number, rows, amount, top, bound, lean):
    order = jax.random.permutation(key, amount)
    heavy_load, common = load_shares(amount, rows * top, bound, lean, True), load_shares(amount, rows * top, bound, lean, False)
    places = jnp.arange(amount)

    def named(lengths, rotation):
        used = int((lengths > 0).sum())
        fixed = max(1, used // 4)
        passed = fixed + (places - fixed + rotation * (used - fixed)) % max(1, amount - fixed)
        return jnp.zeros((amount,), jnp.int32).at[order[jnp.where(places < fixed, places, passed)]].set(jnp.asarray(lengths, jnp.int32))

    lengths = jnp.where(number % 4 == 0, named(heavy_load, number // 4), named(common, number - number // 4 - 1))
    mixed = jax.random.permutation(jax.random.fold_in(own, 3), amount)
    source_of, receiver = mixed[0:amount // 2 * 2:2], mixed[1:amount // 2 * 2:2]
    margin = jnp.minimum(lengths[source_of] - 1, bound - lengths[receiver]) // 2
    margin = jnp.where((source_of == order[0]) | (receiver == order[0]) | (lengths[receiver] == 0), 0, jnp.maximum(margin, 0))
    passed = jax.random.randint(jax.random.fold_in(own, 4), (amount // 2,), 0, 1 << 20) % (margin + 1)
    lengths = lengths.at[source_of].add(-passed).at[receiver].add(passed)
    items = jnp.searchsorted(jnp.cumsum(lengths), jnp.arange(rows * top), side="right").astype(jnp.int32)
    grid = items.reshape(top, rows).T
    grid = grid[jax.random.permutation(jax.random.fold_in(own, 1), rows)]
    rotation = jax.random.randint(jax.random.fold_in(own, 2), (rows, 1), 0, top)
    return jnp.take_along_axis(grid, (jnp.arange(top)[None, :] + rotation) % top, axis=1)


def load_shares(count, total, bound, skew, full):
    loads = [(1 << 20) // math.isqrt(rank ** skew) + 1 for rank in range(1, count + 1)]
    largest = bound if full else min(bound, max(-(-total // count), total * loads[0] // sum(loads)))
    least = 1 if total - largest >= count - 1 else 0
    counts, surplus = [largest] + [least] * (count - 1), total - largest - least * (count - 1)
    while surplus > 0:
        movable = [i for i in range(1, count) if counts[i] < largest] or [i for i in range(1, count) if counts[i] < bound]
        mass, budget = sum([loads[i] for i in movable]), surplus
        for i in movable:
            more = min(bound - counts[i], max(1, budget * loads[i] // mass), surplus)
            counts[i] = counts[i] + more
            surplus = surplus - more
    return np.array(counts)


def normal_values(key, extent, scale, reach, kind=jnp.bfloat16):
    values = scale * jax.random.normal(key, extent, jnp.float32)
    return jnp.clip(values, min=-reach, max=reach).astype(kind)


def setup_inputs(seed: int = 0) -> dict:
    arg_keys = jax.random.split(jax.random.key(seed), 5)
    slc_stack = draw_slc_stack(jax.random.fold_in(arg_keys[4], 71), 0)
    date_pairs = draw_date_pairs(jax.random.fold_in(arg_keys[4], 71), 0)
    pair_owner_keys = jax.random.split(jax.random.fold_in(arg_keys[2], 1), PAIRS // PAIRS)
    pair_owner_turns = jax.random.permutation(jax.random.fold_in(arg_keys[2], 3), PAIRS // PAIRS)
    pair_owner = jax.vmap(lambda own, number: assign_block(jax.random.fold_in(arg_keys[2], 2), own, number, PAIRS, N_ACQ, 1, CAP, 2))(pair_owner_keys, pair_owner_turns).reshape((PAIRS, 1))
    pseudo_inverse = normal_values(arg_keys[3], (ACQS, PAIRS), PAIRS ** -0.5, 0.1875, jnp.float32)
    return {"slc_stack": slc_stack, "date_pairs": date_pairs, "pair_owner": pair_owner, "pseudo_inverse": pseudo_inverse}


def look_average(values):
    shape = values.shape
    grouped = values.reshape(shape[:-1] + (ROWS_DEV // 4, 4, COL_DEV // 16, 16))
    averaged = lax.optimization_barrier(jnp.mean(grouped, axis=(-3, -1)))
    return averaged.reshape(shape[:-1] + (ROWS_DEV // 4 * (COL_DEV // 16),))

def reference(slc_stack, date_pairs, pair_owner, pseudo_inverse):

    def date_power(single):
        real_part = single[0].astype(jnp.float32)
        imag_part = single[1].astype(jnp.float32)
        return look_average(real_part * real_part + imag_part * imag_part) + 1e-06
    power = lax.map(date_power, slc_stack)

    def pair_coherence(pair_row):
        early_slc = slc_stack[pair_row[0]].astype(jnp.float32)
        late_slc = slc_stack[pair_row[1]].astype(jnp.float32)
        cross_real = look_average(early_slc[0] * late_slc[0] + early_slc[1] * late_slc[1])
        cross_imag = look_average(early_slc[1] * late_slc[0] - early_slc[0] * late_slc[1])
        scale_both = jnp.sqrt(power[pair_row[0]] * power[pair_row[1]])
        return jnp.stack([cross_real / scale_both, cross_imag / scale_both], axis=0)
    coherence = lax.map(pair_coherence, date_pairs)
    window_mean = lax.optimization_barrier(jnp.mean(coherence, axis=(2, 3, 4)))
    referenced = coherence - window_mean[:, :, None, None, None]
    num_pairs = date_pairs.shape[0]
    owners = pair_owner[:, 0]
    onehot = (owners[:, None] == jnp.arange(N_ACQ, dtype=jnp.int32)[None, :]).astype(jnp.int32)
    before = jnp.cumsum(onehot, axis=0) - onehot
    ranked = lax.optimization_barrier(jnp.sum(before * onehot, axis=1))
    slot_index = owners * CAP + ranked
    slot_pair = jnp.full((N_ACQ * CAP,), num_pairs, jnp.int32).at[slot_index].set(jnp.arange(num_pairs, dtype=jnp.int32))
    filled = (slot_pair < num_pairs).astype(jnp.float32)
    safe_pair = jnp.minimum(slot_pair, num_pairs - 1)
    taken = jnp.take(referenced, safe_pair, axis=0) * filled[:, None, None, None, None]
    shape = taken.shape
    coherence_slots = taken.reshape(shape[0], shape[1], shape[2], shape[3] * shape[4])
    series_parts = jnp.einsum('ap,pksbl->sbkla', pseudo_inverse, referenced, precision=lax.Precision.HIGHEST, preferred_element_type=jnp.float32)
    return (series_parts, coherence_slots)
```

```python
import jax
import jax.numpy as jnp
from jax import lax
from jax.experimental import pallas as pl
from jax.experimental.pallas import tpu as pltpu
from jax.sharding import PartitionSpec as P

DATES = 256
PAIRS = 1024
OWNERS = 64
CAP = 32
SLOTS = OWNERS * CAP
SPAN = 8
UPPER = 16
LOOKS = 32
LANES = 128
SHORT = 112
VMEM_LIMIT = 50 * 1024 * 1024
F32 = jnp.float32
BF16 = jnp.bfloat16


def dot_nt(left, right):
    return lax.dot_general(
        left, right, (((1,), (1,)), ((), ())), preferred_element_type=F32
    )


def dot_nn(left, right):
    return jnp.dot(left, right, preferred_element_type=F32)


def iota(shape, axis):
    return lax.broadcasted_iota(jnp.int32, shape, axis)


def halves(value):
    high = value.astype(BF16)
    return high, (value - high.astype(F32)).astype(BF16)


def skew(value):
    row = iota(value.shape, 0)
    for bit in (1, 2, 4):
        value = jnp.where((row & bit) != 0, pltpu.roll(value, LANES - bit, 1), value)
    parts = [value[0:8]]
    for start in range(8, value.shape[0], 8):
        parts.append(pltpu.roll(value[start:start + 8], LANES - start, 1))
    return jnp.concatenate(parts, axis=0)


def slot_kernel(dates_ref, owner_ref, pinv_ref, onehot_ref, lag_ref, high_ref, low_ref, table_ref):
    owned = iota((OWNERS, PAIRS), 0) == owner_ref[...]
    earlier = (iota((PAIRS, PAIRS), 0) < iota((PAIRS, PAIRS), 1)).astype(F32).astype(BF16)
    before = dot_nn(owned.astype(F32).astype(BF16), earlier)
    rank = jnp.sum(jnp.where(owned, before, 0.0), axis=0, keepdims=True)
    slot = owner_ref[...] * CAP + rank.astype(jnp.int32)
    early = dates_ref[0:1, :]
    lag = dates_ref[1:2, :] - early
    numbers = jnp.concatenate(
        [
            jnp.broadcast_to((early + 1).astype(F32), (LANES, PAIRS)),
            jnp.broadcast_to(lag.astype(F32), (LANES, PAIRS)),
        ],
        axis=0,
    ).astype(BF16)
    high, low = halves(pinv_ref[...])
    step = 256
    for start in range(0, SLOTS, step):
        rows = slice(start, start + step)
        chosen = (iota((step, PAIRS), 0) + start == slot).astype(F32).astype(BF16)
        found = dot_nt(chosen, numbers)
        wide = jnp.concatenate([found[:, :LANES], found[:, :LANES]], axis=1)
        column = iota((step, DATES), 1).astype(F32) + 1.0
        onehot_ref[rows, :] = (wide == column).astype(F32).astype(BF16)
        lag_ref[rows, :] = found[:, LANES:]
        high_ref[:, rows] = dot_nt(high, chosen).astype(BF16)
        low_ref[:, rows] = dot_nt(low, chosen).astype(BF16)
    for group in range(UPPER // 2):
        shape = (LANES, (SPAN + 1) * LANES)
        row = iota(shape, 0)
        col = iota(shape, 1)
        inner = row // 16
        look = group * 4 + inner // 2
        kind = inner % 2
        want_lag = col // LANES
        want_kind = (col // LOOKS) % 2
        same_kind = jnp.where(want_lag == 0, 0, want_kind) == kind
        match = (row % 16 == want_lag) & (col % LOOKS == look) & same_kind
        table_ref[group * LANES:(group + 1) * LANES, :] = jnp.where(
            match, 1.0 / 64.0, 0.0
        ).astype(BF16)


def coherence_kernel(
    cells_ref, onehot_ref, lag_ref, high_ref, low_ref, table_ref,
    send_ref, series_ref, sum_ref, wide_ref, band_ref, scale_ref,
):
    count = 16
    for start in range(0, DATES, count):
        wide_ref[start * 32:(start + count) * 32, :] = (
            cells_ref[start:start + count].astype(F32).reshape(count * 32, LANES)
        )
    lane = iota((DATES, 2 * LANES), 1)
    zero = jnp.zeros((LANES - 32, 2 * LANES), BF16)
    for group in range(UPPER // 2):
        packed = {}
        for sub in range(2):
            u = group * 2 + sub
            real = wide_ref[pl.ds(u, DATES, stride=32), :]
            imag = wide_ref[pl.ds(UPPER + u, DATES, stride=32), :]
            kinds = (
                jnp.concatenate([real, imag], axis=1).astype(BF16),
                jnp.concatenate([imag, -real], axis=1).astype(BF16),
            )
            sides = [
                jnp.where((lane % 32) // 16 == v, kinds[0].astype(F32), 0.0).astype(BF16)
                for v in range(2)
            ]
            for first in (0, SHORT, 2 * SHORT):
                size = min(SHORT, DATES - first)
                windows = []
                for v in range(2):
                    if first + LANES <= DATES:
                        windows.append(sides[v][first:first + LANES])
                    else:
                        windows.append(jnp.concatenate([sides[v][first:], zero], axis=0))
                spot = iota((size, LANES), 1) - iota((size, LANES), 0)
                for kind in range(2):
                    turned = []
                    for v in range(2):
                        place = 16 * (sub * 4 + v * 2 + kind)
                        window = windows[v]
                        if place:
                            window = jnp.concatenate(
                                [window[LANES - place:], window[:LANES - place]], axis=0
                            )
                        turned.append(window)
                    gram = dot_nt(kinds[kind][first:first + size], jnp.concatenate(turned, axis=0))
                    for v in range(2):
                        place = 16 * (sub * 4 + v * 2 + kind)
                        part = gram[:, v * LANES:(v + 1) * LANES]
                        if first not in packed:
                            packed[first] = part
                        else:
                            inside = ((spot - place) & (LANES - 1)) < 16
                            packed[first] = jnp.where(inside, part, packed[first])
        for first, value in packed.items():
            size = value.shape[0]
            band_ref[first:first + size, group * LANES:(group + 1) * LANES] = skew(value)
    high, low = halves(band_ref[...])
    table = dot_nn(high, table_ref[...]) + dot_nn(low, table_ref[...])
    scale = lax.rsqrt(table[:, :LANES] + 1e-06)
    scale_ref[0:DATES, :] = scale
    scale_ref[DATES:DATES + 8, :] = jnp.zeros((8, LANES), F32)
    left = iota((DATES, LANES), 1) < LANES // 2
    columns = []
    for lag in range(1, SPAN + 1):
        value = table[:, lag * LANES:(lag + 1) * LANES] * scale * scale_ref[lag:lag + DATES, :]
        top = value.astype(BF16).astype(F32)
        columns.append(jnp.where(left, top, value - top).astype(BF16))
    coherence = jnp.concatenate(columns, axis=1)
    step = 256
    pick = ((iota((8, LANES), 1) // LOOKS) % 2 == iota((8, LANES), 0)).astype(F32).astype(BF16)
    series = jnp.zeros((DATES, LANES), F32)
    half = iota((step // CAP, CAP // 2, LANES), 2) < LANES // 2
    for start in range(0, SLOTS, step):
        rows = slice(start, start + step)
        found = dot_nn(onehot_ref[rows, :], coherence)
        lag_of = lag_ref[rows, :]
        value = jnp.zeros((step, LANES), F32)
        for lag in range(1, SPAN + 1):
            value = jnp.where(lag_of == float(lag), found[:, (lag - 1) * LANES:lag * LANES], value)
        exact = value.astype(BF16)
        sum_ref[:, rows] = dot_nt(pick, exact)[0:2]
        series = series + dot_nn(high_ref[:, rows], exact) + dot_nn(low_ref[:, rows], exact)
        value = value + pltpu.roll(value, LANES // 2, 1)
        value = value.reshape(step // CAP, CAP, LANES)
        send_ref[start // CAP:(start + step) // CAP] = jnp.where(
            half, value[:, :CAP // 2], value[:, CAP // 2:]
        )
    series = series + pltpu.roll(series, LANES // 2, 1)
    series_ref[...] = series.T[0:LANES // 2]


def output_kernel(mine_ref, got_ref, sum_ref, series_in_ref, high_ref, low_ref, series_ref, slots_ref):
    total = sum_ref[...] * (1.0 / 8192.0)
    high, low = halves(total)
    mean = (
        dot_nt(high, high_ref[...]) + dot_nt(low, high_ref[...]) + dot_nt(high, low_ref[...])
    )
    for kind in range(2):
        rows = slice(kind * LOOKS, (kind + 1) * LOOKS)
        series_ref[rows, :] = series_in_ref[rows, :] - mean[kind:kind + 1, :]
    own = iota((CAP, SLOTS), 1) == iota((CAP, SLOTS), 0) + mine_ref[0] * CAP
    means = [
        jnp.sum(jnp.where(own, total[kind:kind + 1, :], 0.0), axis=1, keepdims=True)
        for kind in range(2)
    ]
    chunk = iota((CAP // 2, LANES), 1) // LOOKS
    for block in range(OWNERS // 4):
        parts = [got_ref[4 * block + j] for j in range(4)]
        for t in range(4):
            side, kind = t // 2, t % 2
            result = None
            for j in range(4):
                turn = (LOOKS * (j - t)) % LANES
                moved = pltpu.roll(parts[j], turn, 1) if turn else parts[j]
                result = moved if result is None else jnp.where(chunk == j, moved, result)
            rows = slice(side * CAP // 2, (side + 1) * CAP // 2)
            slots_ref[rows, kind, block * LANES:(block + 1) * LANES] = result - means[kind][rows]


def vmem(number):
    return [pl.BlockSpec(memory_space=pltpu.VMEM)] * number


def params():
    return pltpu.CompilerParams(vmem_limit_bytes=VMEM_LIMIT)


def exchange_sum(value):
    for axis, steps in (("acq", (1,)), ("strip", (1, 2)), ("acq", (2, 4, 8, 16, 32))):
        size = lax.axis_size(axis)
        for step in steps:
            value = value + lax.ppermute(value, axis, [(i, i ^ step) for i in range(size)])
    return value


def on_device(slc_stack, date_pairs, pair_owner, pseudo_inverse):
    sent = slc_stack.reshape(4, 2, OWNERS, UPPER, LANES).transpose(2, 0, 1, 3, 4)
    cells = lax.all_to_all(
        sent.reshape(OWNERS, LANES, LANES), "acq", split_axis=0, concat_axis=0, tiled=True
    )
    shape = jax.ShapeDtypeStruct
    onehot, lag, high, low, table = pl.pallas_call(
        slot_kernel,
        out_shape=(
            shape((SLOTS, DATES), BF16),
            shape((SLOTS, LANES), F32),
            shape((DATES, SLOTS), BF16),
            shape((DATES, SLOTS), BF16),
            shape((UPPER // 2 * LANES, (SPAN + 1) * LANES), BF16),
        ),
        in_specs=vmem(3),
        out_specs=tuple(vmem(5)),
        compiler_params=params(),
        name="slot_order",
        cost_estimate=pl.CostEstimate(
            flops=4_000_000_000, bytes_accessed=8_000_000, transcendentals=0
        ),
    )(date_pairs.T, pair_owner.T, pseudo_inverse)
    packed, series, sums = pl.pallas_call(
        coherence_kernel,
        out_shape=(
            shape((OWNERS, CAP // 2, LANES), F32),
            shape((2 * LOOKS, DATES), F32),
            shape((2, SLOTS), F32),
        ),
        in_specs=vmem(6),
        out_specs=tuple(vmem(3)),
        scratch_shapes=[
            pltpu.VMEM((DATES * 32, LANES), F32),
            pltpu.VMEM((DATES, UPPER // 2 * LANES), F32),
            pltpu.VMEM((DATES + 8, LANES), F32),
        ],
        compiler_params=params(),
        name="coherence",
        cost_estimate=pl.CostEstimate(
            flops=6_000_000_000, bytes_accessed=8_000_000, transcendentals=0
        ),
    )(cells.reshape(DATES, 32, LANES), onehot, lag, high, low, table)
    got = lax.all_to_all(packed, "acq", split_axis=0, concat_axis=0, tiled=True)
    total = exchange_sum(sums)
    mine = lax.axis_index("acq").astype(jnp.int32).reshape(1)
    series, slots = pl.pallas_call(
        output_kernel,
        out_shape=(
            shape((2 * LOOKS, DATES), F32),
            shape((CAP, 2, OWNERS * LOOKS), F32),
        ),
        in_specs=[pl.BlockSpec(memory_space=pltpu.SMEM)] + vmem(5),
        out_specs=tuple(vmem(2)),
        compiler_params=params(),
        name="referenced",
    )(mine, got, total, series, high, low)
    return (
        series.reshape(1, 1, 2, LOOKS, DATES),
        slots.reshape(CAP, 2, 1, OWNERS * LOOKS),
    )


def solution(mesh):
    placed = (P("acq", None, "strip", None, None), P(), P(), P())
    return jax.shard_map(
        on_device,
        mesh=mesh,
        in_specs=placed,
        out_specs=(P("strip", "acq", None, None, None), P("acq", None, "strip", None)),
        check_vma=False,
    )
```

```python
import jax
import jax.numpy as jnp
from jax import lax
from jax.experimental import pallas as pl
from jax.experimental.pallas import tpu as pltpu
from jax.sharding import PartitionSpec as P

DATES = 256
PAIRS = 1024
OWNERS = 64
CAP = 32
SLOTS = OWNERS * CAP
SPAN = 8
UPPER = 16
LOOKS = 32
LANES = 128
ENTRIES = SPAN * DATES
PLANE = 8
OWN = 4 * PLANE
INNER = OWN - SPAN
TOGETHER = 8
ROWS = CAP // 2 + 1
TABLE = (1 + SPAN // 2) * LANES
VMEM_LIMIT = 20 * 1024 * 1024
F32 = jnp.float32
BF16 = jnp.bfloat16


def dot_nt(left, right):
    return lax.dot_general(
        left, right, (((1,), (1,)), ((), ())), preferred_element_type=F32
    )


def dot_nn(left, right):
    return jnp.dot(left, right, preferred_element_type=F32)


def iota(shape, axis):
    return lax.broadcasted_iota(jnp.int32, shape, axis)


def halves(value):
    high = value.astype(BF16)
    return high, (value - high.astype(F32)).astype(BF16)


def flags(mask):
    return mask.astype(F32).astype(BF16)


def skew_rows(band_ref, dates):
    for start in range(0, band_ref.shape[1], LANES):
        value = band_ref[:, start:start + LANES]
        row = iota(value.shape, 0)
        for bit in (1, 2, 4):
            value = jnp.where((row & bit) != 0, pltpu.roll(value, LANES - bit, 1), value)
        parts = []
        for first in range(0, value.shape[0], 8):
            turn = first % dates
            part = value[first:first + 8]
            parts.append(pltpu.roll(part, LANES - turn, 1) if turn else part)
        band_ref[:, start:start + LANES] = jnp.concatenate(parts, axis=0)


def cell_row(date, kind, u):
    return (u // 4) * 32 + date * 8 + (u % 4) * 2 + kind


def pack_kernel(image_ref, sent_ref, wide_ref):
    blocks = image_ref.shape[1]
    pitch = wide_ref.shape[0] // blocks
    for part in range(8):
        for u in range(UPPER):
            row = cell_row(part // 2, part % 2, u)
            wide_ref[pl.ds(row, blocks, stride=pitch), :] = image_ref[
                part, :, u * LANES:(u + 1) * LANES
            ].astype(F32)
    for block in range(blocks):
        sent_ref[block % PLANE, block // PLANE] = wide_ref[
            block * pitch:block * pitch + LANES, :
        ].astype(BF16)


def slot_kernel(
    mine_ref, dates_ref, owner_ref, pinv_ref,
    code_ref, own_early_ref, own_lag_ref, high_ref, low_ref, table_ref,
):
    owned = iota((OWNERS, PAIRS), 0) == owner_ref[...]
    earlier = flags(iota((PAIRS, PAIRS), 0) < iota((PAIRS, PAIRS), 1))
    before = dot_nn(flags(owned), earlier)
    rank = jnp.sum(jnp.where(owned, before, 0.0), axis=0, keepdims=True)
    slot = owner_ref[...] * CAP + rank.astype(jnp.int32)
    early = dates_ref[0:1, :]
    lag = dates_ref[1:2, :] - early
    entry = (lag - 1) * DATES + early
    numbers = jnp.concatenate(
        [
            jnp.broadcast_to((early + 1).astype(F32), (LANES, PAIRS)),
            jnp.broadcast_to(lag.astype(F32), (LANES, PAIRS)),
        ],
        axis=0,
    ).astype(BF16)
    found = dot_nt(flags(iota((CAP, PAIRS), 0) + mine_ref[0] * CAP == slot), numbers)
    wide = jnp.concatenate([found[:, :LANES], found[:, :LANES]], axis=1)
    own_early_ref[...] = (wide == iota((CAP, DATES), 1).astype(F32) + 1.0).astype(F32)
    own_lag_ref[...] = found[:, LANES:]
    high, low = halves(pinv_ref[...])
    step = 256
    for start in range(0, SLOTS, step):
        rows = slice(start, start + step)
        place = iota((step, PAIRS), 0) + start
        code = dot_nt(numbers, flags(place == slot))
        code_ref[0:8, rows] = code[0:8]
        code_ref[8:16, rows] = code[LANES:LANES + 8]
        chosen = flags(place == entry)
        weight = dot_nt(high, chosen) + dot_nt(low, chosen)
        high_ref[:, rows], low_ref[:, rows] = halves(weight)
    for block in range(8):
        shape = (LANES, TABLE)
        row = iota(shape, 0)
        col = iota(shape, 1)
        inner = row // 16
        look = (block // 2) * 8 + (inner % 4) * 2 + inner // 4
        lag_of = jnp.where(col < LANES, 0, col // (LANES // 2) - 1)
        kind = jnp.where(col < LANES, 0, (col // LOOKS) % 2)
        match = (row % 16 == lag_of) & (col % LOOKS == look) & (kind == block % 2)
        table_ref[block * LANES:(block + 1) * LANES, :] = jnp.where(
            match, 1.0 / 64.0, 0.0
        ).astype(BF16)


def window_masks():
    side_of = (iota((1, 2 * LANES), 1) % 32) // 16
    return [flags(side_of == v) for v in range(2)]


def band_blocks(wide_ref, slot, quarter, dates, keep, store):
    gap = jnp.zeros((LANES // 2 - dates, 2 * LANES), BF16)
    spot = iota((dates, LANES), 1) - (iota((dates, LANES), 0) & -8)
    packed = [None, None]
    for sub in range(4):
        real = wide_ref[slot, pl.ds(2 * sub, dates, stride=8), :]
        imag = wide_ref[slot, pl.ds(2 * sub + 1, dates, stride=8), :]
        straight = jnp.concatenate([real, imag], axis=1).astype(BF16)
        crossed = jnp.concatenate([imag, -real], axis=1).astype(BF16)
        window = jnp.concatenate([straight * keep[0], gap, straight * keep[1], gap], axis=0)
        if sub:
            cut = LANES - 16 * sub
            window = jnp.concatenate([window[cut:], window[:cut]], axis=0)
        gram = dot_nt(jnp.concatenate([straight, crossed], axis=0), window)
        inside = ((spot - 16 * sub) & (LANES // 2 - 1)) < 16
        for kind in range(2):
            part = gram[kind * dates:(kind + 1) * dates]
            packed[kind] = jnp.where(inside, part, packed[kind]) if sub else part
    for kind in range(2):
        store((quarter * 2 + kind) * LANES, packed[kind])


def edge_blocks(wide_ref, slot, quarter, keep, store):
    dates = 2 * SPAN
    straight, crossed = [], []
    for sub in range(4):
        real = wide_ref[slot, pl.ds(2 * sub, dates, stride=8), :]
        imag = wide_ref[slot, pl.ds(2 * sub + 1, dates, stride=8), :]
        straight.append(jnp.concatenate([real, imag], axis=1).astype(BF16))
        crossed.append(jnp.concatenate([imag, -real], axis=1).astype(BF16))
    whole = jnp.concatenate(straight, axis=0)
    window = jnp.concatenate([whole * keep[0], whole * keep[1]], axis=0)
    gram = dot_nt(jnp.concatenate([whole] + crossed, axis=0), window)
    sub_of = (iota((dates, LANES), 1) // 16) % 4
    for kind in range(2):
        value = None
        for sub in range(4):
            start = (kind * 4 + sub) * dates
            part = gram[start:start + dates]
            value = part if value is None else jnp.where(sub_of == sub, part, value)
        store((quarter * 2 + kind) * LANES, value)


def normalised(band_ref, table_ref, scale_ref):
    count = band_ref.shape[0]
    high, low = halves(band_ref[...])
    table = dot_nn(high, table_ref[...]) + dot_nn(low, table_ref[...])
    scale = lax.rsqrt(table[:, :LANES] + 1e-06)
    scale_ref[0:count, :] = scale
    scale_ref[count:count + 8, :] = jnp.zeros((8, LANES), F32)
    left = iota((count, LANES), 1) < LANES // 2
    for pair in range(SPAN // 2):
        lag = 2 * pair + 1
        late = jnp.where(left, scale_ref[lag:lag + count, :], scale_ref[lag + 1:lag + 1 + count, :])
        yield pair, table[:, (pair + 1) * LANES:(pair + 2) * LANES] * scale * late


def window_sums(total):
    pick = flags(iota((8, LANES), 1) // LOOKS == iota((8, LANES), 0))
    high, low = halves(jnp.concatenate([total] * 4, axis=0))
    return (dot_nt(pick, high) + dot_nt(pick, low))[0:4]


def each_tile(tile):
    def body(index, carry):
        for part in range(TOGETHER):
            tile(index * TOGETHER + part, 4 * part)
        return carry

    lax.fori_loop(0, PLANE // TOGETHER, body, 0)


def inner_kernel(
    cells_ref, table_ref, out_ref, sum_ref, table_copy_ref, wide_ref, band_ref, scale_ref
):
    keep = window_masks()

    def tile(index, slot):
        for quarter in range(4):
            rows = slice(quarter * 32, (quarter + 1) * 32)
            wide_ref[slot + quarter] = cells_ref[:, index, rows, :].astype(F32).reshape(OWN * 8, LANES)

            def store(start, value):
                place = pl.ds(pl.multiple_of(index * OWN, OWN), OWN)
                band_ref[place, start:start + LANES] = value

            band_blocks(wide_ref, slot + quarter, quarter, OWN, keep, store)

    each_tile(tile)
    skew_rows(band_ref, OWN)
    table_copy_ref[...] = table_ref[...]
    rest = jnp.zeros((SPAN, LANES), F32)
    for pair, value in normalised(band_ref, table_ref, scale_ref):
        total = jnp.zeros((INNER, LANES), F32)
        for index in range(PLANE):
            part = value[index * OWN:index * OWN + INNER]
            out_ref[index, :, pair * LANES:(pair + 1) * LANES] = part
            total = total + part
        sum_ref[4 * pair:4 * pair + 4, :] = window_sums(jnp.concatenate([total, rest], axis=0))


def edge_kernel(
    cells_ref, halo_ref, table_ref, inner_ref, inner_sum_ref, out_ref, sum_ref,
    wide_ref, band_ref, scale_ref,
):
    keep = window_masks()
    count = 2 * SPAN

    def tile(index, slot):
        for quarter in range(4):
            rows = slice(quarter * 32, (quarter + 1) * 32)
            wide_ref[slot + quarter, 0:SPAN * 8] = (
                cells_ref[:, index, rows, :].astype(F32).reshape(SPAN * 8, LANES)
            )
            wide_ref[slot + quarter, SPAN * 8:] = (
                halo_ref[:, index, rows, :].astype(F32).reshape(SPAN * 8, LANES)
            )

            def store(start, value):
                place = pl.ds(pl.multiple_of(index * count, count), count)
                band_ref[place, start:start + LANES] = value

            edge_blocks(wide_ref, slot + quarter, quarter, keep, store)

    each_tile(tile)
    skew_rows(band_ref, count)
    out_ref[:, 0:INNER, :] = inner_ref[...]
    rest = jnp.zeros((INNER, LANES), F32)
    for pair, value in normalised(band_ref, table_ref, scale_ref):
        total = jnp.zeros((SPAN, LANES), F32)
        for index in range(PLANE):
            part = value[index * count:index * count + SPAN]
            out_ref[index, INNER:, pair * LANES:(pair + 1) * LANES] = part
            total = total + part
        rows = slice(4 * pair, 4 * pair + 4)
        sums = window_sums(jnp.concatenate([rest, total], axis=0))
        sum_ref[rows, :] = inner_sum_ref[rows, :] + sums


def split_table(table_ref):
    left = iota((DATES, LANES), 1) < LANES // 2
    columns = []
    for pair in range(SPAN // 2):
        value = table_ref[:, pair * LANES:(pair + 1) * LANES]
        top = value.astype(BF16).astype(F32)
        rest = pltpu.roll(value - top, LANES // 2, 1)
        columns.append(jnp.where(left, top, rest).astype(BF16))
        columns.append(jnp.where(left, rest, top).astype(BF16))
    return columns


def select_kernel(mine_ref, table_ref, code_ref, sum_ref, send_ref):
    coherence = jnp.concatenate(split_table(table_ref), axis=1)
    wanted = 2 * (mine_ref[0] % PLANE) + iota((2 * SPAN, LANES), 1) // OWN
    extra = jnp.where(iota((2 * SPAN, LANES), 0) == wanted, sum_ref[...], 0.0)
    extra = jnp.sum(extra, axis=0, keepdims=True)
    step = 256
    half = iota((CAP // 2, LANES), 1) < LANES // 2
    column = iota((step, DATES), 1).astype(F32) + 1.0
    for start in range(0, SLOTS, step):
        rows = slice(start, start + step)
        early = jnp.broadcast_to(code_ref[0:1, rows], (LANES, step)).T
        lag_of = jnp.broadcast_to(code_ref[8:9, rows], (LANES, step)).T
        onehot = flags(jnp.concatenate([early, early], axis=1) == column)
        found = dot_nn(onehot, coherence)
        value = jnp.zeros((step, LANES), F32)
        for lag in range(1, SPAN + 1):
            value = jnp.where(lag_of == float(lag), found[:, (lag - 1) * LANES:lag * LANES], value)
        value = value + pltpu.roll(value, LANES // 2, 1)
        for part in range(step // CAP):
            first = part * CAP
            middle = first + CAP // 2
            target = (start // CAP + part) * ROWS
            send_ref[target:target + CAP // 2, :] = jnp.where(
                half, value[first:middle], value[middle:first + CAP]
            )
            send_ref[target + CAP // 2:target + ROWS, :] = extra


def series_kernel(table_ref, high_ref, low_ref, series_ref):
    columns = split_table(table_ref)
    series = jnp.zeros((DATES, LANES), F32)
    for lag in range(SPAN):
        rows = slice(lag * DATES, (lag + 1) * DATES)
        series = series + dot_nn(high_ref[:, rows], columns[lag])
        series = series + dot_nn(low_ref[:, rows], columns[lag])
    series = series + pltpu.roll(series, LANES // 2, 1)
    series_ref[...] = series.T[0:LANES // 2]


def output_kernel(
    got_ref, high_ref, low_ref, own_early_ref, own_lag_ref, series_in_ref, series_ref, slots_ref
):
    sums = got_ref[pl.ds(ROWS - 1, OWNERS, stride=ROWS), :] * (1.0 / 8192.0)
    group = iota((SPAN, LANES), 1) // OWN
    totals = []
    for kind in range(2):
        lanes = []
        for block in range(2):
            value = jnp.zeros((SPAN, LANES), F32)
            for j in range(4):
                plane = block * 4 + j
                part = sums[plane * PLANE:(plane + 1) * PLANE]
                turn = (OWN * (j - kind)) % LANES
                part = pltpu.roll(part, turn, 1) if turn else part
                value = jnp.where(group == j, part, value)
            lanes.append(value)
        totals.append(jnp.concatenate(lanes, axis=1))
    high, low = halves(jnp.concatenate(totals, axis=0))
    lag_of = own_lag_ref[:, 0:1]
    shift = [jnp.zeros((1, DATES), F32) for _ in range(2)]
    found = [jnp.zeros((CAP, DATES), F32) for _ in range(2)]
    for lag in range(SPAN):
        rows = slice(lag * DATES, (lag + 1) * DATES)
        part = (
            dot_nt(high, high_ref[:, rows])
            + dot_nt(low, high_ref[:, rows])
            + dot_nt(high, low_ref[:, rows])
        )
        for kind in range(2):
            row = SPAN * kind + lag
            shift[kind] = shift[kind] + part[row:row + 1]
            found[kind] = jnp.where(
                lag_of == float(lag + 1), totals[kind][lag:lag + 1], found[kind]
            )
    means = []
    for kind in range(2):
        rows = slice(kind * LOOKS, (kind + 1) * LOOKS)
        series_ref[rows, :] = series_in_ref[rows, :] - shift[kind]
        means.append(jnp.sum(found[kind] * own_early_ref[...], axis=1, keepdims=True))
    chunk = iota((CAP // 2, LANES), 1) // LOOKS
    for block in range(OWNERS // 4):
        parts = [
            got_ref[(4 * block + j) * ROWS:(4 * block + j) * ROWS + CAP // 2, :] for j in range(4)
        ]
        for t in range(4):
            side, kind = t // 2, t % 2
            result = None
            for j in range(4):
                turn = (LOOKS * (j - t)) % LANES
                moved = pltpu.roll(parts[j], turn, 1) if turn else parts[j]
                result = moved if result is None else jnp.where(chunk == j, moved, result)
            rows = slice(side * CAP // 2, (side + 1) * CAP // 2)
            first = (side * CAP + kind) * (OWNERS // 4) + block
            slots_ref[pl.ds(first, CAP // 2, stride=OWNERS // 2), :] = result - means[kind][rows]


def vmem(number):
    return [pl.BlockSpec(memory_space=pltpu.VMEM)] * number


def params():
    return pltpu.CompilerParams(vmem_limit_bytes=VMEM_LIMIT)


def cost(flops, size):
    return pl.CostEstimate(flops=flops, bytes_accessed=size, transcendentals=0)


def along(value, axis_groups):
    return lax.all_to_all(
        value, "acq", split_axis=0, concat_axis=0, tiled=True, axis_index_groups=axis_groups
    )


def exchange_sum(value):
    for axis, steps in (("acq", (1,)), ("acq", (2, 4, 6)), ("strip", (1, 2, 3))):
        size = lax.axis_size(axis)
        moved = [
            lax.ppermute(value, axis, [(i, i ^ step) for i in range(size)]) for step in steps
        ]
        for part in moved:
            value = value + part
    return value


SHAPE = jax.ShapeDtypeStruct
SCALAR = [pl.BlockSpec(memory_space=pltpu.SMEM)]


def pack(slc_stack):
    batch = 2 * PLANE
    return pl.pallas_call(
        pack_kernel,
        grid=(OWNERS // batch,),
        out_shape=SHAPE((PLANE, PLANE, LANES, LANES), BF16),
        in_specs=[pl.BlockSpec((8, batch, UPPER * LANES), lambda i: (0, i, 0))],
        out_specs=pl.BlockSpec((PLANE, 2, LANES, LANES), lambda i: (0, i, 0, 0)),
        scratch_shapes=[pltpu.VMEM((batch * (LANES + 4), LANES), F32)],
        compiler_params=params(),
        name="pack",
    )(slc_stack.reshape(8, OWNERS, UPPER * LANES))


def slot_order(mine, date_pairs, pair_owner, pseudo_inverse):
    return pl.pallas_call(
        slot_kernel,
        out_shape=(
            SHAPE((16, SLOTS), F32),
            SHAPE((CAP, DATES), F32),
            SHAPE((CAP, LANES), F32),
            SHAPE((DATES, ENTRIES), BF16),
            SHAPE((DATES, ENTRIES), BF16),
            SHAPE((8 * LANES, TABLE), BF16),
        ),
        in_specs=SCALAR + vmem(3),
        out_specs=tuple(vmem(6)),
        compiler_params=params(),
        name="slot_order",
        cost_estimate=cost(4_000_000_000, 8_000_000),
    )(mine, date_pairs.T, pair_owner.T, pseudo_inverse)


def inner_coherence(cells, table):
    return pl.pallas_call(
        inner_kernel,
        out_shape=(
            SHAPE((PLANE, INNER, SPAN * 2 * LOOKS), F32),
            SHAPE((2 * SPAN, LANES), F32),
            SHAPE(table.shape, BF16),
        ),
        in_specs=vmem(2),
        out_specs=tuple(vmem(3)),
        scratch_shapes=[
            pltpu.VMEM((4 * TOGETHER, OWN * 8, LANES), F32),
            pltpu.VMEM((PLANE * OWN, 8 * LANES), F32),
            pltpu.VMEM((PLANE * OWN + 8, LANES), F32),
        ],
        compiler_params=params(),
        name="coherence",
        cost_estimate=cost(4_000_000_000, 8_000_000),
    )(cells, table)


def edge_coherence(cells, halo, table, inner, inner_sums):
    return pl.pallas_call(
        edge_kernel,
        out_shape=(
            SHAPE((PLANE, OWN, SPAN * 2 * LOOKS), F32),
            SHAPE((2 * SPAN, LANES), F32),
        ),
        in_specs=vmem(5),
        out_specs=tuple(vmem(2)),
        scratch_shapes=[
            pltpu.VMEM((4 * TOGETHER, 2 * SPAN * 8, LANES), F32),
            pltpu.VMEM((PLANE * 2 * SPAN, 8 * LANES), F32),
            pltpu.VMEM((PLANE * 2 * SPAN + 8, LANES), F32),
        ],
        compiler_params=params(),
        name="edge",
        cost_estimate=cost(2_000_000_000, 4_000_000),
    )(cells, halo, table, inner, inner_sums)


def select(mine, coherence, code, sums):
    return pl.pallas_call(
        select_kernel,
        out_shape=SHAPE((OWNERS * ROWS, LANES), F32),
        in_specs=SCALAR + vmem(3),
        out_specs=vmem(1)[0],
        compiler_params=params(),
        name="select",
        cost_estimate=cost(2_000_000_000, 4_000_000),
    )(mine, coherence, code, sums)


def invert(coherence, high, low):
    return pl.pallas_call(
        series_kernel,
        out_shape=SHAPE((2 * LOOKS, DATES), F32),
        in_specs=vmem(3),
        out_specs=vmem(1)[0],
        compiler_params=params(),
        name="series",
        cost_estimate=cost(1_000_000_000, 3_000_000),
    )(coherence, high, low)


def output(got, high, low, own_early, own_lag, series):
    return pl.pallas_call(
        output_kernel,
        out_shape=(SHAPE((2 * LOOKS, DATES), F32), SHAPE((CAP * 2 * UPPER, LANES), F32)),
        in_specs=vmem(6),
        out_specs=tuple(vmem(2)),
        compiler_params=params(),
        name="referenced",
    )(got, high, low, own_early, own_lag, series)


def on_device(slc_stack, date_pairs, pair_owner, pseudo_inverse):
    size = lax.axis_size("acq")
    planes = [list(range(start, start + PLANE)) for start in range(0, size, PLANE)]
    pillars = [list(range(start, size, PLANE)) for start in range(PLANE)]
    mine = lax.axis_index("acq").astype(jnp.int32).reshape(1)
    cells = along(pack(slc_stack), planes)
    ordered = slot_order(mine, date_pairs, pair_owner, pseudo_inverse)
    cells, ordered = lax.optimization_barrier((cells, ordered))
    code, own_early, own_lag, high, low, table = ordered
    halo = lax.ppermute(cells[0:2], "acq", [(i, (i - PLANE) % size) for i in range(size)])
    inner, sums, table = inner_coherence(cells, table)
    parts, sums = edge_coherence(cells[PLANE - 2:], halo, table, inner, sums)
    coherence = along(parts, pillars).reshape(DATES, SPAN * 2 * LOOKS)
    packed = select(mine, coherence, code, exchange_sum(sums))
    got = lax.all_to_all(
        packed.reshape(OWNERS, 1, ROWS * LANES), "acq", split_axis=0, concat_axis=0, tiled=True
    ).reshape(OWNERS * ROWS, LANES)
    series = invert(coherence, high, low)
    series, slots = output(got, high, low, own_early, own_lag, series)
    return (
        series.reshape(1, 1, 2, LOOKS, DATES),
        slots.reshape(CAP, 2, 1, OWNERS * LOOKS),
    )


def solution(mesh):
    placed = (P("acq", None, "strip", None, None), P(), P(), P())
    return jax.shard_map(
        on_device,
        mesh=mesh,
        in_specs=placed,
        out_specs=(P("strip", "acq", None, None, None), P("acq", None, "strip", None)),
        check_vma=False,
    )
```

```python
import jax
import jax.numpy as jnp
from jax import lax
from jax.experimental import pallas as pl
from jax.experimental.pallas import tpu as pltpu
from jax.sharding import PartitionSpec as P

DATES = 256
PAIRS = 1024
OWNERS = 64
CAP = 32
SLOTS = OWNERS * CAP
SPAN = 8
UPPER = 16
LOOKS = 32
LANES = 128
ENTRIES = SPAN * DATES
PLANE = 8
OWN = 4 * PLANE
INNER = OWN - SPAN
TOGETHER = 8
ROWS = CAP // 2 + 2
PLANE_ORDER = (0, 2, 4, 6, 1, 3, 5, 7)
PLANE_PLACE = tuple(PLANE_ORDER.index(w) for w in range(PLANE))
PILLAR_ORDER = (0, 3, 6, 1, 4, 7, 2, 5)
PILLAR_PLACE = tuple(PILLAR_ORDER.index(z) for z in range(PLANE))
TABLE = (1 + SPAN // 2) * LANES
VMEM_LIMIT = 20 * 1024 * 1024
WIDE_LIMIT = 58 * 1024 * 1024
F32 = jnp.float32
BF16 = jnp.bfloat16


def dot_nt(left, right):
    return lax.dot_general(
        left, right, (((1,), (1,)), ((), ())), preferred_element_type=F32
    )


def dot_nn(left, right):
    return jnp.dot(left, right, preferred_element_type=F32)


def iota(shape, axis):
    return lax.broadcasted_iota(jnp.int32, shape, axis)


def halves(value):
    high = value.astype(BF16)
    return high, (value - high.astype(F32)).astype(BF16)


def flags(mask):
    return mask.astype(F32).astype(BF16)


def skew_rows(band_ref, dates):
    for start in range(0, band_ref.shape[1], LANES):
        value = band_ref[:, start:start + LANES]
        row = iota(value.shape, 0)
        for bit in (1, 2, 4):
            value = jnp.where((row & bit) != 0, pltpu.roll(value, LANES - bit, 1), value)
        parts = []
        for first in range(0, value.shape[0], 8):
            turn = first % dates
            part = value[first:first + 8]
            parts.append(pltpu.roll(part, LANES - turn, 1) if turn else part)
        band_ref[:, start:start + LANES] = jnp.concatenate(parts, axis=0)


def cell_row(date, kind, u):
    return (u // 4) * 32 + date * 8 + (u % 4) * 2 + kind


def pack_kernel(image_ref, sent_ref, held_ref, wide_ref, ready_ref, come_sem, gone_sem):
    batch = 2 * PLANE
    pitch = LANES + 4
    chunks = OWNERS // batch
    coming, going = [], []
    for chunk in range(chunks):
        rows = pl.ds(chunk * batch, batch)
        copy = pltpu.make_async_copy(
            image_ref.at[:, rows, :], held_ref.at[:, rows, :], come_sem.at[chunk]
        )
        copy.start()
        coming.append(copy)
    for chunk in range(chunks):
        coming[chunk].wait()
        rows = slice(chunk * batch, (chunk + 1) * batch)
        for part in range(8):
            for u in range(UPPER):
                row = cell_row(part // 2, part % 2, u)
                wide_ref[chunk % 2, pl.ds(row, batch, stride=pitch), :] = held_ref[
                    part, rows, u * LANES:(u + 1) * LANES
                ].astype(F32)
        for block in range(batch):
            ready_ref[PLANE_PLACE[block % PLANE], 2 * chunk + block // PLANE] = wide_ref[
                chunk % 2, block * pitch:block * pitch + LANES, :
            ].astype(BF16)
        tiles = pl.ds(2 * chunk, 2)
        copy = pltpu.make_async_copy(
            ready_ref.at[:, tiles], sent_ref.at[:, tiles], gone_sem.at[chunk]
        )
        copy.start()
        going.append(copy)
    for copy in going:
        copy.wait()


def slot_kernel(
    mine_ref, dates_ref, owner_ref, pinv_ref,
    code_ref, own_early_ref, own_lag_ref, high_ref, low_ref, table_ref,
):
    owned = iota((OWNERS, PAIRS), 0) == owner_ref[...]
    earlier = flags(iota((PAIRS, PAIRS), 0) < iota((PAIRS, PAIRS), 1))
    before = dot_nn(flags(owned), earlier)
    rank = jnp.sum(jnp.where(owned, before, 0.0), axis=0, keepdims=True)
    slot = owner_ref[...] * CAP + rank.astype(jnp.int32)
    early = dates_ref[0:1, :]
    lag = dates_ref[1:2, :] - early
    entry = (lag - 1) * DATES + early
    numbers = jnp.concatenate(
        [
            jnp.broadcast_to((early + 1).astype(F32), (LANES, PAIRS)),
            jnp.broadcast_to(lag.astype(F32), (LANES, PAIRS)),
        ],
        axis=0,
    ).astype(BF16)
    found = dot_nt(flags(iota((CAP, PAIRS), 0) + mine_ref[0] * CAP == slot), numbers)
    wide = jnp.concatenate([found[:, :LANES], found[:, :LANES]], axis=1)
    own_early_ref[...] = (wide == iota((CAP, DATES), 1).astype(F32) + 1.0).astype(F32)
    own_lag_ref[...] = found[:, LANES:]
    high, low = halves(pinv_ref[...])
    step = 256
    for start in range(0, SLOTS, step):
        rows = slice(start, start + step)
        place = iota((step, PAIRS), 0) + start
        code = dot_nt(numbers, flags(place == slot))
        code_ref[0:8, rows] = code[0:8]
        code_ref[8:16, rows] = code[LANES:LANES + 8]
        chosen = flags(place == entry)
        weight = dot_nt(high, chosen) + dot_nt(low, chosen)
        high_ref[:, rows], low_ref[:, rows] = halves(weight)
    for block in range(8):
        shape = (LANES, TABLE)
        row = iota(shape, 0)
        col = iota(shape, 1)
        inner = row // 16
        look = (block // 2) * 8 + (inner % 4) * 2 + inner // 4
        lag_of = jnp.where(col < LANES, 0, col // (LANES // 2) - 1)
        kind = jnp.where(col < LANES, 0, (col // LOOKS) % 2)
        match = (row % 16 == lag_of) & (col % LOOKS == look) & (kind == block % 2)
        table_ref[block * LANES:(block + 1) * LANES, :] = jnp.where(
            match, 1.0 / 64.0, 0.0
        ).astype(BF16)


def window_masks():
    side_of = (iota((1, 2 * LANES), 1) % 32) // 16
    return [flags(side_of == v) for v in range(2)]


def band_blocks(wide_ref, slot, quarter, dates, keep, store):
    gap = jnp.zeros((LANES // 2 - dates, 2 * LANES), BF16)
    spot = iota((dates, LANES), 1) - (iota((dates, LANES), 0) & -8)
    packed = [None, None]
    for sub in range(4):
        real = wide_ref[slot, pl.ds(2 * sub, dates, stride=8), :]
        imag = wide_ref[slot, pl.ds(2 * sub + 1, dates, stride=8), :]
        straight = jnp.concatenate([real, imag], axis=1).astype(BF16)
        crossed = jnp.concatenate([imag, -real], axis=1).astype(BF16)
        window = jnp.concatenate([straight * keep[0], gap, straight * keep[1], gap], axis=0)
        if sub:
            cut = LANES - 16 * sub
            window = jnp.concatenate([window[cut:], window[:cut]], axis=0)
        gram = dot_nt(jnp.concatenate([straight, crossed], axis=0), window)
        inside = ((spot - 16 * sub) & (LANES // 2 - 1)) < 16
        for kind in range(2):
            part = gram[kind * dates:(kind + 1) * dates]
            packed[kind] = jnp.where(inside, part, packed[kind]) if sub else part
    for kind in range(2):
        store((quarter * 2 + kind) * LANES, packed[kind])


def edge_blocks(wide_ref, slot, quarter, keep, store):
    dates = 2 * SPAN
    straight, crossed = [], []
    for sub in range(4):
        real = wide_ref[slot, pl.ds(2 * sub, dates, stride=8), :]
        imag = wide_ref[slot, pl.ds(2 * sub + 1, dates, stride=8), :]
        straight.append(jnp.concatenate([real, imag], axis=1).astype(BF16))
        crossed.append(jnp.concatenate([imag, -real], axis=1).astype(BF16))
    whole = jnp.concatenate(straight, axis=0)
    window = jnp.concatenate([whole * keep[0], whole * keep[1]], axis=0)
    gram = dot_nt(jnp.concatenate([whole] + crossed, axis=0), window)
    sub_of = (iota((dates, LANES), 1) // 16) % 4
    for kind in range(2):
        value = None
        for sub in range(4):
            start = (kind * 4 + sub) * dates
            part = gram[start:start + dates]
            value = part if value is None else jnp.where(sub_of == sub, part, value)
        store((quarter * 2 + kind) * LANES, value)


def normalised(band_ref, table_ref, scale_ref):
    count = band_ref.shape[0]
    high, low = halves(band_ref[...])
    table = dot_nn(high, table_ref[...]) + dot_nn(low, table_ref[...])
    scale = lax.rsqrt(table[:, :LANES] + 1e-06)
    scale_ref[0:count, :] = scale
    scale_ref[count:count + 8, :] = jnp.zeros((8, LANES), F32)
    left = iota((count, LANES), 1) < LANES // 2
    for pair in range(SPAN // 2):
        lag = 2 * pair + 1
        late = jnp.where(left, scale_ref[lag:lag + count, :], scale_ref[lag + 1:lag + 1 + count, :])
        yield pair, table[:, (pair + 1) * LANES:(pair + 2) * LANES] * scale * late


def window_sums(total):
    pick = flags(iota((8, LANES), 1) // LOOKS == iota((8, LANES), 0))
    high, low = halves(jnp.concatenate([total] * 4, axis=0))
    return (dot_nt(pick, high) + dot_nt(pick, low))[0:4]


def each_tile(tile):
    def body(index, carry):
        for part in range(TOGETHER):
            tile(index * TOGETHER + part, 4 * part)
        return carry

    lax.fori_loop(0, PLANE // TOGETHER, body, 0)


def inner_kernel(
    cells_ref, table_ref, out_ref, sum_ref, table_copy_ref, wide_ref, band_ref, scale_ref
):
    keep = window_masks()

    def tile(index, slot):
        for quarter in range(4):
            rows = slice(quarter * 32, (quarter + 1) * 32)
            for w in range(PLANE):
                wide_ref[slot + quarter, w * 32:(w + 1) * 32] = cells_ref[
                    PLANE_PLACE[w], index, rows, :
                ].astype(F32)

            def store(start, value):
                place = pl.ds(pl.multiple_of(index * OWN, OWN), OWN)
                band_ref[place, start:start + LANES] = value

            band_blocks(wide_ref, slot + quarter, quarter, OWN, keep, store)

    each_tile(tile)
    skew_rows(band_ref, OWN)
    table_copy_ref[...] = table_ref[...]
    rest = jnp.zeros((SPAN, LANES), F32)
    for pair, value in normalised(band_ref, table_ref, scale_ref):
        total = jnp.zeros((INNER, LANES), F32)
        for index in range(PLANE):
            part = value[index * OWN:index * OWN + INNER]
            out_ref[PILLAR_PLACE[index], pair * INNER:(pair + 1) * INNER, :] = part
            total = total + part
        sum_ref[4 * pair:4 * pair + 4, :] = window_sums(jnp.concatenate([total, rest], axis=0))


def edge_kernel(
    cells_ref, halo_ref, table_ref, inner_ref, inner_sum_ref, out_ref, sum_ref,
    wide_ref, band_ref, scale_ref,
):
    keep = window_masks()
    count = 2 * SPAN

    def tile(index, slot):
        for quarter in range(4):
            rows = slice(quarter * 32, (quarter + 1) * 32)
            wide_ref[slot + quarter, 0:SPAN * 8] = (
                cells_ref[:, index, rows, :].astype(F32).reshape(SPAN * 8, LANES)
            )
            wide_ref[slot + quarter, SPAN * 8:] = (
                halo_ref[:, index, rows, :].astype(F32).reshape(SPAN * 8, LANES)
            )

            def store(start, value):
                place = pl.ds(pl.multiple_of(index * count, count), count)
                band_ref[place, start:start + LANES] = value

            edge_blocks(wide_ref, slot + quarter, quarter, keep, store)

    each_tile(tile)
    skew_rows(band_ref, count)
    for pair in range(SPAN // 2):
        out_ref[:, pair * OWN:pair * OWN + INNER, :] = inner_ref[
            :, pair * INNER:(pair + 1) * INNER, :
        ]
    rest = jnp.zeros((INNER, LANES), F32)
    for pair, value in normalised(band_ref, table_ref, scale_ref):
        total = jnp.zeros((SPAN, LANES), F32)
        for index in range(PLANE):
            part = value[index * count:index * count + SPAN]
            out_ref[PILLAR_PLACE[index], pair * OWN + INNER:(pair + 1) * OWN, :] = part
            total = total + part
        rows = slice(4 * pair, 4 * pair + 4)
        sums = window_sums(jnp.concatenate([rest, total], axis=0))
        sum_ref[rows, :] = inner_sum_ref[rows, :] + sums


def split_table(table_ref):
    left = iota((DATES, LANES), 1) < LANES // 2
    columns = []
    for pair in range(SPAN // 2):
        rows = slice(pair * OWN, (pair + 1) * OWN)
        value = jnp.concatenate([table_ref[place, rows, :] for place in PILLAR_PLACE], axis=0)
        top = value.astype(BF16).astype(F32)
        rest = pltpu.roll(value - top, LANES // 2, 1)
        columns.append(jnp.where(left, top, rest).astype(BF16))
        columns.append(jnp.where(left, rest, top).astype(BF16))
    return columns


def select_kernel(mine_ref, table_ref, code_ref, sum_ref, send_ref):
    coherence = jnp.concatenate(split_table(table_ref), axis=1)
    row = iota((2 * SPAN, LANES), 0) - SPAN * (mine_ref[0] % 2)
    extra = []
    for part in range(2):
        wanted = row == 4 * part + iota((2 * SPAN, LANES), 1) // OWN
        extra.append(jnp.sum(jnp.where(wanted, sum_ref[...], 0.0), axis=0, keepdims=True))
    extra = jnp.concatenate(extra, axis=0)
    step = 256
    half = iota((CAP // 2, LANES), 1) < LANES // 2
    column = iota((step, DATES), 1).astype(F32) + 1.0
    for start in range(0, SLOTS, step):
        rows = slice(start, start + step)
        early = jnp.broadcast_to(code_ref[0:1, rows], (LANES, step)).T
        lag_of = jnp.broadcast_to(code_ref[8:9, rows], (LANES, step)).T
        onehot = flags(jnp.concatenate([early, early], axis=1) == column)
        found = dot_nn(onehot, coherence)
        value = jnp.zeros((step, LANES), F32)
        for lag in range(1, SPAN + 1):
            value = jnp.where(lag_of == float(lag), found[:, (lag - 1) * LANES:lag * LANES], value)
        value = value + pltpu.roll(value, LANES // 2, 1)
        for part in range(step // CAP):
            first = part * CAP
            middle = first + CAP // 2
            target = (start // CAP + part) * ROWS
            send_ref[target:target + CAP // 2, :] = jnp.where(
                half, value[first:middle], value[middle:first + CAP]
            )
            send_ref[target + CAP // 2:target + ROWS, :] = extra


def series_kernel(table_ref, high_ref, low_ref, series_ref):
    columns = split_table(table_ref)
    series = jnp.zeros((DATES, LANES), F32)
    for lag in range(SPAN):
        rows = slice(lag * DATES, (lag + 1) * DATES)
        series = series + dot_nn(high_ref[:, rows], columns[lag])
        series = series + dot_nn(low_ref[:, rows], columns[lag])
    series = series + pltpu.roll(series, LANES // 2, 1)
    series_ref[...] = series.T[0:LANES // 2]


def output_kernel(
    got_ref, high_ref, low_ref, own_early_ref, own_lag_ref, series_in_ref, series_ref, slots_ref
):
    group = iota((PLANE, LANES), 1) // OWN
    placed = {}
    for part in range(2):
        sums = got_ref[pl.ds(CAP // 2 + part, OWNERS, stride=ROWS), :] * (1.0 / 8192.0)
        for plane in range(PLANE):
            value = sums[plane * PLANE:(plane + 1) * PLANE]
            value = value + pltpu.roll(value, 4, 0)
            value = value + pltpu.roll(value, 2, 0)
            for j in range(4):
                turn = (OWN * (plane - j)) % LANES
                moved = pltpu.roll(value, turn, 1) if turn else value
                key = part, j, plane // 4
                placed[key] = jnp.where(group == plane % 4, moved, placed[key]) if key in placed else moved
    rows = [
        jnp.concatenate([placed[part, j, 0], placed[part, j, 1]], axis=1)[core:core + 1]
        for core in range(2) for part in range(2) for j in range(4)
    ]
    total = jnp.concatenate(rows, axis=0)
    high, low = halves(total)
    lag_of = own_lag_ref[:, 0:1]
    shift = [jnp.zeros((1, DATES), F32) for _ in range(2)]
    found = [jnp.zeros((CAP, DATES), F32) for _ in range(2)]
    for lag in range(SPAN):
        rows = slice(lag * DATES, (lag + 1) * DATES)
        part = (
            dot_nt(high, high_ref[:, rows])
            + dot_nt(low, high_ref[:, rows])
            + dot_nt(high, low_ref[:, rows])
        )
        for kind in range(2):
            row = 2 * lag + kind
            shift[kind] = shift[kind] + part[row:row + 1]
            found[kind] = jnp.where(lag_of == float(lag + 1), total[row:row + 1], found[kind])
    means = []
    for kind in range(2):
        rows = slice(kind * LOOKS, (kind + 1) * LOOKS)
        series_ref[rows, :] = series_in_ref[rows, :] - shift[kind]
        means.append(jnp.sum(found[kind] * own_early_ref[...], axis=1, keepdims=True))
    chunk = iota((CAP // 2, LANES), 1) // LOOKS
    for block in range(OWNERS // 4):
        parts = [
            got_ref[(4 * block + j) * ROWS:(4 * block + j) * ROWS + CAP // 2, :] for j in range(4)
        ]
        for t in range(4):
            side, kind = t // 2, t % 2
            result = None
            for j in range(4):
                turn = (LOOKS * (j - t)) % LANES
                moved = pltpu.roll(parts[j], turn, 1) if turn else parts[j]
                result = moved if result is None else jnp.where(chunk == j, moved, result)
            rows = slice(side * CAP // 2, (side + 1) * CAP // 2)
            first = (side * CAP + kind) * (OWNERS // 4) + block
            slots_ref[pl.ds(first, CAP // 2, stride=OWNERS // 2), :] = result - means[kind][rows]


def vmem(number):
    return [pl.BlockSpec(memory_space=pltpu.VMEM)] * number


def params(limit=VMEM_LIMIT):
    return pltpu.CompilerParams(vmem_limit_bytes=limit)


def cost(flops, size):
    return pl.CostEstimate(flops=flops, bytes_accessed=size, transcendentals=0)


def along(value, axis_groups):
    return lax.all_to_all(
        value, "acq", split_axis=0, concat_axis=0, tiled=True, axis_index_groups=axis_groups
    )


def exchange_sum(value):
    for axis, steps in (("acq", (1,)), ("strip", (1, 2, 3))):
        size = lax.axis_size(axis)
        moved = [
            lax.ppermute(value, axis, [(i, i ^ step) for i in range(size)]) for step in steps
        ]
        for part in moved:
            value = value + part
    return value


SHAPE = jax.ShapeDtypeStruct
SCALAR = [pl.BlockSpec(memory_space=pltpu.SMEM)]


def pack(slc_stack):
    batch = 2 * PLANE
    return pl.pallas_call(
        pack_kernel,
        out_shape=SHAPE((PLANE, PLANE, LANES, LANES), BF16),
        in_specs=[pl.BlockSpec(memory_space=pl.ANY)],
        out_specs=pl.BlockSpec(memory_space=pl.ANY),
        scratch_shapes=[
            pltpu.VMEM((8, OWNERS, UPPER * LANES), BF16),
            pltpu.VMEM((2, batch * (LANES + 4), LANES), F32),
            pltpu.VMEM((PLANE, PLANE, LANES, LANES), BF16),
            pltpu.SemaphoreType.DMA((OWNERS // batch,)),
            pltpu.SemaphoreType.DMA((OWNERS // batch,)),
        ],
        compiler_params=params(WIDE_LIMIT),
        name="pack",
    )(slc_stack.reshape(8, OWNERS, UPPER * LANES))


def slot_order(mine, date_pairs, pair_owner, pseudo_inverse):
    return pl.pallas_call(
        slot_kernel,
        out_shape=(
            SHAPE((16, SLOTS), F32),
            SHAPE((CAP, DATES), F32),
            SHAPE((CAP, LANES), F32),
            SHAPE((DATES, ENTRIES), BF16),
            SHAPE((DATES, ENTRIES), BF16),
            SHAPE((8 * LANES, TABLE), BF16),
        ),
        in_specs=SCALAR + vmem(3),
        out_specs=tuple(vmem(6)),
        compiler_params=params(),
        name="slot_order",
        cost_estimate=cost(4_000_000_000, 8_000_000),
    )(mine, date_pairs.T, pair_owner.T, pseudo_inverse)


def inner_coherence(cells, table):
    return pl.pallas_call(
        inner_kernel,
        out_shape=(
            SHAPE((PLANE, SPAN // 2 * INNER, LANES), F32),
            SHAPE((2 * SPAN, LANES), F32),
            SHAPE(table.shape, BF16),
        ),
        in_specs=vmem(2),
        out_specs=tuple(vmem(3)),
        scratch_shapes=[
            pltpu.VMEM((4 * TOGETHER, OWN * 8, LANES), F32),
            pltpu.VMEM((PLANE * OWN, 8 * LANES), F32),
            pltpu.VMEM((PLANE * OWN + 8, LANES), F32),
        ],
        compiler_params=params(),
        name="coherence",
        cost_estimate=cost(4_000_000_000, 8_000_000),
    )(cells, table)


def edge_coherence(cells, halo, table, inner, inner_sums):
    return pl.pallas_call(
        edge_kernel,
        out_shape=(
            SHAPE((PLANE, SPAN // 2 * OWN, LANES), F32),
            SHAPE((2 * SPAN, LANES), F32),
        ),
        in_specs=vmem(5),
        out_specs=tuple(vmem(2)),
        scratch_shapes=[
            pltpu.VMEM((4 * TOGETHER, 2 * SPAN * 8, LANES), F32),
            pltpu.VMEM((PLANE * 2 * SPAN, 8 * LANES), F32),
            pltpu.VMEM((PLANE * 2 * SPAN + 8, LANES), F32),
        ],
        compiler_params=params(),
        name="edge",
        cost_estimate=cost(2_000_000_000, 4_000_000),
    )(cells, halo, table, inner, inner_sums)


def select(mine, coherence, code, sums):
    return pl.pallas_call(
        select_kernel,
        out_shape=SHAPE((OWNERS * ROWS, LANES), F32),
        in_specs=SCALAR + vmem(3),
        out_specs=vmem(1)[0],
        compiler_params=params(),
        name="select",
        cost_estimate=cost(2_000_000_000, 4_000_000),
    )(mine, coherence, code, sums)


def invert(coherence, high, low):
    return pl.pallas_call(
        series_kernel,
        out_shape=SHAPE((2 * LOOKS, DATES), F32),
        in_specs=vmem(3),
        out_specs=vmem(1)[0],
        compiler_params=params(WIDE_LIMIT),
        name="series",
        cost_estimate=cost(1_000_000_000, 3_000_000),
    )(coherence, high, low)


def output(got, high, low, own_early, own_lag, series):
    return pl.pallas_call(
        output_kernel,
        out_shape=(SHAPE((2 * LOOKS, DATES), F32), SHAPE((CAP * 2 * UPPER, LANES), F32)),
        in_specs=vmem(6),
        out_specs=tuple(vmem(2)),
        compiler_params=params(),
        name="referenced",
    )(got, high, low, own_early, own_lag, series)


def on_device(slc_stack, date_pairs, pair_owner, pseudo_inverse):
    size = lax.axis_size("acq")
    planes = [[start + w for w in PLANE_ORDER] for start in range(0, size, PLANE)]
    pillars = [[start + PLANE * z for z in PILLAR_ORDER] for start in range(PLANE)]
    mine = lax.axis_index("acq").astype(jnp.int32).reshape(1)
    cells = along(pack(slc_stack), planes)
    ordered = slot_order(mine, date_pairs, pair_owner, pseudo_inverse)
    cells, ordered = lax.optimization_barrier((cells, ordered))
    code, own_early, own_lag, high, low, table = ordered
    first, last = (cells[PLANE_PLACE[w]:PLANE:PLANE // 2] for w in (0, PLANE - 2))
    halo = lax.ppermute(first, "acq", [(i, (i - PLANE) % size) for i in range(size)])
    inner, sums, table = inner_coherence(cells, table)
    parts, sums = edge_coherence(last, halo, table, inner, sums)
    coherence = along(parts, pillars)
    packed = select(mine, coherence, code, exchange_sum(sums))
    got = lax.all_to_all(
        packed.reshape(OWNERS, 1, ROWS * LANES), "acq", split_axis=0, concat_axis=0, tiled=True
    ).reshape(OWNERS * ROWS, LANES)
    series = invert(coherence, high, low)
    series, slots = output(got, high, low, own_early, own_lag, series)
    return (
        series.reshape(1, 1, 2, LOOKS, DATES),
        slots.reshape(CAP, 2, 1, OWNERS * LOOKS),
    )


def solution(mesh):
    placed = (P("acq", None, "strip", None, None), P(), P(), P())
    return jax.shard_map(
        on_device,
        mesh=mesh,
        in_specs=placed,
        out_specs=(P("strip", "acq", None, None, None), P("acq", None, "strip", None)),
        check_vma=False,
    )
```

```python
import jax
import jax.numpy as jnp
from jax import lax
from jax.experimental import pallas as pl
from jax.experimental.pallas import tpu as pltpu
from jax.sharding import PartitionSpec as P

DATES = 256
PAIRS = 1024
OWNERS = 64
CAP = 32
SLOTS = OWNERS * CAP
SPAN = 8
UPPER = 16
LOOKS = 32
LANES = 128
ENTRIES = SPAN * DATES
PLANE = 8
OWN = 4 * PLANE
INNER = OWN - SPAN
TOGETHER = 8
ROWS = CAP // 2 + 3
HALF = PLANE // 2
PLANE_ORDER = (0, 2, 4, 6, 1, 3, 5, 7)
PLANE_PLACE = tuple(PLANE_ORDER.index(w) for w in range(PLANE))
PILLAR_ORDER = (0, 3, 6, 1, 4, 7, 2, 5)
PILLAR_PLACE = tuple(PILLAR_ORDER.index(z) for z in range(PLANE))
TABLE = (1 + SPAN // 2) * LANES
VMEM_LIMIT = 20 * 1024 * 1024
WIDE_LIMIT = 58 * 1024 * 1024
F32 = jnp.float32
BF16 = jnp.bfloat16


def dot_nt(left, right):
    return lax.dot_general(
        left, right, (((1,), (1,)), ((), ())), preferred_element_type=F32
    )


def dot_nn(left, right):
    return jnp.dot(left, right, preferred_element_type=F32)


def iota(shape, axis):
    return lax.broadcasted_iota(jnp.int32, shape, axis)


def halves(value):
    high = value.astype(BF16)
    return high, (value - high.astype(F32)).astype(BF16)


def flags(mask):
    return mask.astype(F32).astype(BF16)


def skew_rows(band_ref, dates):
    for start in range(0, band_ref.shape[1], LANES):
        value = band_ref[:, start:start + LANES]
        row = iota(value.shape, 0)
        for bit in (1, 2, 4):
            value = jnp.where((row & bit) != 0, pltpu.roll(value, LANES - bit, 1), value)
        parts = []
        for first in range(0, value.shape[0], 8):
            turn = first % dates
            part = value[first:first + 8]
            parts.append(pltpu.roll(part, LANES - turn, 1) if turn else part)
        band_ref[:, start:start + LANES] = jnp.concatenate(parts, axis=0)


def cell_row(date, kind, u):
    return (u // 4) * 32 + date * 8 + (u % 4) * 2 + kind


def pack_kernel(image_ref, sent_ref, held_ref, wide_ref, ready_ref, come_sem, gone_sem):
    batch = 2 * PLANE
    pitch = LANES + 4
    chunks = OWNERS // batch
    coming, going = [], []
    for chunk in range(chunks):
        rows = pl.ds(chunk * batch, batch)
        copy = pltpu.make_async_copy(
            image_ref.at[:, rows, :], held_ref.at[:, rows, :], come_sem.at[chunk]
        )
        copy.start()
        coming.append(copy)
    for chunk in range(chunks):
        coming[chunk].wait()
        rows = slice(chunk * batch, (chunk + 1) * batch)
        for part in range(8):
            for u in range(UPPER):
                row = cell_row(part // 2, part % 2, u)
                wide_ref[chunk % 2, pl.ds(row, batch, stride=pitch), :] = held_ref[
                    part, rows, u * LANES:(u + 1) * LANES
                ].astype(F32)
        for block in range(batch):
            ready_ref[PLANE_PLACE[block % PLANE], 2 * chunk + block // PLANE] = wide_ref[
                chunk % 2, block * pitch:block * pitch + LANES, :
            ].astype(BF16)
        tiles = pl.ds(2 * chunk, 2)
        copy = pltpu.make_async_copy(
            ready_ref.at[:, tiles], sent_ref.at[:, tiles], gone_sem.at[chunk]
        )
        copy.start()
        going.append(copy)
    for copy in going:
        copy.wait()


def slot_kernel(
    mine_ref, dates_ref, owner_ref, pinv_ref,
    code_ref, own_early_ref, own_lag_ref, high_ref, low_ref, table_ref,
):
    owned = iota((OWNERS, PAIRS), 0) == owner_ref[...]
    earlier = flags(iota((PAIRS, PAIRS), 0) < iota((PAIRS, PAIRS), 1))
    before = dot_nn(flags(owned), earlier)
    rank = jnp.sum(jnp.where(owned, before, 0.0), axis=0, keepdims=True)
    slot = owner_ref[...] * CAP + rank.astype(jnp.int32)
    early = dates_ref[0:1, :]
    lag = dates_ref[1:2, :] - early
    entry = (lag - 1) * DATES + early
    numbers = jnp.concatenate(
        [
            jnp.broadcast_to((early + 1).astype(F32), (LANES, PAIRS)),
            jnp.broadcast_to(lag.astype(F32), (LANES, PAIRS)),
        ],
        axis=0,
    ).astype(BF16)
    found = dot_nt(flags(iota((CAP, PAIRS), 0) + mine_ref[0] * CAP == slot), numbers)
    wide = jnp.concatenate([found[:, :LANES], found[:, :LANES]], axis=1)
    own_early_ref[...] = (wide == iota((CAP, DATES), 1).astype(F32) + 1.0).astype(F32)
    own_lag_ref[...] = found[:, LANES:]
    high, low = halves(pinv_ref[...])
    step = 256
    for start in range(0, SLOTS, step):
        rows = slice(start, start + step)
        place = iota((step, PAIRS), 0) + start
        code = dot_nt(numbers, flags(place == slot))
        code_ref[0:8, rows] = code[0:8]
        code_ref[8:16, rows] = code[LANES:LANES + 8]
        chosen = flags(place == entry)
        weight = dot_nt(high, chosen) + dot_nt(low, chosen)
        high_ref[:, rows], low_ref[:, rows] = halves(weight)
    for block in range(8):
        shape = (LANES, TABLE)
        row = iota(shape, 0)
        col = iota(shape, 1)
        inner = row // 16
        look = (block // 2) * 8 + (inner % 4) * 2 + inner // 4
        lag_of = jnp.where(col < LANES, 0, col // (LANES // 2) - 1)
        kind = jnp.where(col < LANES, 0, (col // LOOKS) % 2)
        match = (row % 16 == lag_of) & (col % LOOKS == look) & (kind == block % 2)
        table_ref[block * LANES:(block + 1) * LANES, :] = jnp.where(
            match, 1.0 / 64.0, 0.0
        ).astype(BF16)


def window_masks():
    side_of = (iota((1, 2 * LANES), 1) % 32) // 16
    return [flags(side_of == v) for v in range(2)]


def band_blocks(wide_ref, slot, quarter, dates, keep, store):
    gap = jnp.zeros((LANES // 2 - dates, 2 * LANES), BF16)
    spot = iota((dates, LANES), 1) - (iota((dates, LANES), 0) & -8)
    packed = [None, None]
    for sub in range(4):
        real = wide_ref[slot, pl.ds(2 * sub, dates, stride=8), :]
        imag = wide_ref[slot, pl.ds(2 * sub + 1, dates, stride=8), :]
        straight = jnp.concatenate([real, imag], axis=1).astype(BF16)
        crossed = jnp.concatenate([imag, -real], axis=1).astype(BF16)
        window = jnp.concatenate([straight * keep[0], gap, straight * keep[1], gap], axis=0)
        if sub:
            cut = LANES - 16 * sub
            window = jnp.concatenate([window[cut:], window[:cut]], axis=0)
        gram = dot_nt(jnp.concatenate([straight, crossed], axis=0), window)
        inside = ((spot - 16 * sub) & (LANES // 2 - 1)) < 16
        for kind in range(2):
            part = gram[kind * dates:(kind + 1) * dates]
            packed[kind] = jnp.where(inside, part, packed[kind]) if sub else part
    for kind in range(2):
        store((quarter * 2 + kind) * LANES, packed[kind])


def edge_blocks(wide_ref, slot, quarter, keep, store):
    dates = 2 * SPAN
    straight, crossed = [], []
    for sub in range(4):
        real = wide_ref[slot, pl.ds(2 * sub, dates, stride=8), :]
        imag = wide_ref[slot, pl.ds(2 * sub + 1, dates, stride=8), :]
        straight.append(jnp.concatenate([real, imag], axis=1).astype(BF16))
        crossed.append(jnp.concatenate([imag, -real], axis=1).astype(BF16))
    whole = jnp.concatenate(straight, axis=0)
    window = jnp.concatenate([whole * keep[0], whole * keep[1]], axis=0)
    gram = dot_nt(jnp.concatenate([whole] + crossed, axis=0), window)
    sub_of = (iota((dates, LANES), 1) // 16) % 4
    for kind in range(2):
        value = None
        for sub in range(4):
            start = (kind * 4 + sub) * dates
            part = gram[start:start + dates]
            value = part if value is None else jnp.where(sub_of == sub, part, value)
        store((quarter * 2 + kind) * LANES, value)


def normalised(band_ref, table_ref, scale_ref):
    count = band_ref.shape[0]
    high, low = halves(band_ref[...])
    table = dot_nn(high, table_ref[...]) + dot_nn(low, table_ref[...])
    scale = lax.rsqrt(table[:, :LANES] + 1e-06)
    scale_ref[0:count, :] = scale
    scale_ref[count:count + 8, :] = jnp.zeros((8, LANES), F32)
    left = iota((count, LANES), 1) < LANES // 2
    for pair in range(SPAN // 2):
        lag = 2 * pair + 1
        late = jnp.where(left, scale_ref[lag:lag + count, :], scale_ref[lag + 1:lag + 1 + count, :])
        yield pair, table[:, (pair + 1) * LANES:(pair + 2) * LANES] * scale * late


def window_sums(total):
    pick = flags(iota((8, LANES), 1) // LOOKS == iota((8, LANES), 0))
    high, low = halves(jnp.concatenate([total] * (LANES // total.shape[0]), axis=0))
    return (dot_nt(pick, high) + dot_nt(pick, low))[0:4]


def each_tile(tile):
    def body(index, carry):
        for part in range(TOGETHER):
            tile(index * TOGETHER + part, 4 * part)
        return carry

    lax.fori_loop(0, PLANE // TOGETHER, body, 0)


def inner_kernel(
    cells_ref, table_ref, out_ref, sum_ref, table_copy_ref, wide_ref, band_ref, scale_ref
):
    keep = window_masks()

    def tile(index, slot):
        for quarter in range(4):
            rows = slice(quarter * 32, (quarter + 1) * 32)
            for w in range(PLANE):
                wide_ref[slot + quarter, w * 32:(w + 1) * 32] = cells_ref[
                    PLANE_PLACE[w], index, rows, :
                ].astype(F32)

            def store(start, value):
                place = pl.ds(pl.multiple_of(index * OWN, OWN), OWN)
                band_ref[place, start:start + LANES] = value

            band_blocks(wide_ref, slot + quarter, quarter, OWN, keep, store)

    each_tile(tile)
    skew_rows(band_ref, OWN)
    table_copy_ref[...] = table_ref[...]
    rest = jnp.zeros((SPAN, LANES), F32)
    for pair, value in normalised(band_ref, table_ref, scale_ref):
        total = jnp.zeros((INNER, LANES), F32)
        for index in range(PLANE):
            part = value[index * OWN:index * OWN + INNER]
            out_ref[PILLAR_PLACE[index], pair * INNER:(pair + 1) * INNER, :] = part
            total = total + part
        sum_ref[4 * pair:4 * pair + 4, :] = window_sums(jnp.concatenate([total, rest], axis=0))


def edge_kernel(
    last_ref, next_ref, before_ref, first_ref, table_ref, inner_ref, inner_sum_ref,
    out_ref, sum_ref, wide_ref, band_ref, scale_ref,
):
    keep = window_masks()
    count = 2 * SPAN
    for index in range(PLANE):
        early_ref, late_ref = (last_ref, next_ref) if index < HALF else (before_ref, first_ref)
        for quarter in range(4):
            slot = 4 * index + quarter
            rows = slice(quarter * 32, (quarter + 1) * 32)
            for part, source in enumerate((early_ref, late_ref)):
                wide_ref[slot, part * SPAN * 8:(part + 1) * SPAN * 8] = (
                    source[:, index % HALF, rows, :].astype(F32).reshape(SPAN * 8, LANES)
                )

            def store(start, value):
                band_ref[index * count:(index + 1) * count, start:start + LANES] = value

            edge_blocks(wide_ref, slot, quarter, keep, store)
    skew_rows(band_ref, count)
    rest = jnp.zeros((INNER, LANES), F32)
    for pair, value in normalised(band_ref, table_ref, scale_ref):
        totals = [jnp.zeros((SPAN, LANES), F32), jnp.zeros((SPAN, LANES), F32)]
        for index in range(PLANE):
            part = value[index * count:index * count + SPAN]
            out_ref[PILLAR_PLACE[index], pair * OWN + INNER:(pair + 1) * OWN, :] = part
            totals[index // HALF] = totals[index // HALF] + part
        out_ref[:, pair * OWN:pair * OWN + INNER, :] = inner_ref[
            :, pair * INNER:(pair + 1) * INNER, :
        ]
        rows = slice(4 * pair, 4 * pair + 4)
        sums = window_sums(jnp.concatenate([rest, totals[0]], axis=0))
        sum_ref[rows, :] = inner_sum_ref[rows, :] + sums
        sum_ref[2 * SPAN + 4 * pair:2 * SPAN + 4 * pair + 4, :] = window_sums(totals[1])


def split_table(mine_ref, table_ref):
    upper = mine_ref[0] // PLANE >= HALF
    left = iota((DATES, LANES), 1) < LANES // 2
    columns = []
    for pair in range(SPAN // 2):
        inner = slice(pair * OWN, pair * OWN + INNER)
        edge = slice(pair * OWN + INNER, (pair + 1) * OWN)
        parts = []
        for plane in range(PLANE):
            parts.append(table_ref[PILLAR_PLACE[plane], inner, :])
            same = table_ref[PILLAR_PLACE[plane], edge, :]
            after = table_ref[PILLAR_PLACE[(plane + 1) % PLANE], edge, :]
            parts.append(jnp.where(upper, after, same))
        value = jnp.concatenate(parts, axis=0)
        top = value.astype(BF16).astype(F32)
        rest = pltpu.roll(value - top, LANES // 2, 1)
        columns.append(jnp.where(left, top, rest).astype(BF16))
        columns.append(jnp.where(left, rest, top).astype(BF16))
    return columns


def select_kernel(mine_ref, table_ref, code_ref, sum_ref, send_ref):
    coherence = jnp.concatenate(split_table(mine_ref, table_ref), axis=1)
    row = iota((2 * SPAN, LANES), 0) - SPAN * (mine_ref[0] % 2)
    extra = []
    for part in range(2):
        wanted = row == 4 * part + iota((2 * SPAN, LANES), 1) // OWN
        extra.append(jnp.sum(jnp.where(wanted, sum_ref[0:2 * SPAN], 0.0), axis=0, keepdims=True))
    wanted = row == iota((2 * SPAN, LANES), 1) // SPAN
    extra.append(jnp.sum(jnp.where(wanted, sum_ref[2 * SPAN:], 0.0), axis=0, keepdims=True))
    extra = jnp.concatenate(extra, axis=0)
    step = 256
    half = iota((CAP // 2, LANES), 1) < LANES // 2
    column = iota((step, DATES), 1).astype(F32) + 1.0
    for start in range(0, SLOTS, step):
        rows = slice(start, start + step)
        early = jnp.broadcast_to(code_ref[0:1, rows], (LANES, step)).T
        lag_of = jnp.broadcast_to(code_ref[8:9, rows], (LANES, step)).T
        onehot = flags(jnp.concatenate([early, early], axis=1) == column)
        found = dot_nn(onehot, coherence)
        value = jnp.zeros((step, LANES), F32)
        for lag in range(1, SPAN + 1):
            value = jnp.where(lag_of == float(lag), found[:, (lag - 1) * LANES:lag * LANES], value)
        value = value + pltpu.roll(value, LANES // 2, 1)
        for part in range(step // CAP):
            first = part * CAP
            middle = first + CAP // 2
            target = (start // CAP + part) * ROWS
            send_ref[target:target + CAP // 2, :] = jnp.where(
                half, value[first:middle], value[middle:first + CAP]
            )
            send_ref[target + CAP // 2:target + ROWS, :] = extra


def series_kernel(mine_ref, table_ref, high_ref, low_ref, series_ref):
    columns = split_table(mine_ref, table_ref)
    series = jnp.zeros((DATES, LANES), F32)
    for lag in range(SPAN):
        rows = slice(lag * DATES, (lag + 1) * DATES)
        series = series + dot_nn(high_ref[:, rows], columns[lag])
        series = series + dot_nn(low_ref[:, rows], columns[lag])
    series = series + pltpu.roll(series, LANES // 2, 1)
    series_ref[...] = series.T[0:LANES // 2]


def output_kernel(
    got_ref, high_ref, low_ref, own_early_ref, own_lag_ref, series_in_ref, series_ref, slots_ref
):
    group = iota((PLANE, LANES), 1) // OWN
    placed = {}
    for part in range(2):
        sums = got_ref[pl.ds(CAP // 2 + part, OWNERS, stride=ROWS), :] * (1.0 / 8192.0)
        for plane in range(PLANE):
            value = sums[plane * PLANE:(plane + 1) * PLANE]
            value = value + pltpu.roll(value, 4, 0)
            value = value + pltpu.roll(value, 2, 0)
            for j in range(4):
                turn = (OWN * (plane - j)) % LANES
                moved = pltpu.roll(value, turn, 1) if turn else value
                key = part, j, plane // 4
                placed[key] = jnp.where(group == plane % 4, moved, placed[key]) if key in placed else moved
    group = iota((PLANE, LANES), 1) // SPAN
    sums = got_ref[pl.ds(CAP // 2 + 2, OWNERS, stride=ROWS), :] * (1.0 / 8192.0)
    for plane in range(PLANE):
        value = sums[plane * PLANE:(plane + 1) * PLANE]
        value = value + pltpu.roll(value, 4, 0)
        value = value + pltpu.roll(value, 2, 0)
        target = (plane - 1) % PLANE
        spot = (target % 4) * 4 + 3
        for row in range(SPAN):
            turn = SPAN * (spot - row) % LANES
            moved = pltpu.roll(value, turn, 1) if turn else value
            key = row // 4, row % 4, target // 4
            placed[key] = placed[key] + jnp.where(group == spot, moved, 0.0)
    rows = [
        jnp.concatenate([placed[part, j, 0], placed[part, j, 1]], axis=1)[core:core + 1]
        for core in range(2) for part in range(2) for j in range(4)
    ]
    total = jnp.concatenate(rows, axis=0)
    high, low = halves(total)
    lag_of = own_lag_ref[:, 0:1]
    shift = [jnp.zeros((1, DATES), F32) for _ in range(2)]
    found = [jnp.zeros((CAP, DATES), F32) for _ in range(2)]
    for lag in range(SPAN):
        rows = slice(lag * DATES, (lag + 1) * DATES)
        part = (
            dot_nt(high, high_ref[:, rows])
            + dot_nt(low, high_ref[:, rows])
            + dot_nt(high, low_ref[:, rows])
        )
        for kind in range(2):
            row = 2 * lag + kind
            shift[kind] = shift[kind] + part[row:row + 1]
            found[kind] = jnp.where(lag_of == float(lag + 1), total[row:row + 1], found[kind])
    means = []
    for kind in range(2):
        rows = slice(kind * LOOKS, (kind + 1) * LOOKS)
        series_ref[rows, :] = series_in_ref[rows, :] - shift[kind]
        means.append(jnp.sum(found[kind] * own_early_ref[...], axis=1, keepdims=True))
    chunk = iota((CAP // 2, LANES), 1) // LOOKS
    for block in range(OWNERS // 4):
        parts = [
            got_ref[(4 * block + j) * ROWS:(4 * block + j) * ROWS + CAP // 2, :] for j in range(4)
        ]
        for t in range(4):
            side, kind = t // 2, t % 2
            result = None
            for j in range(4):
                turn = (LOOKS * (j - t)) % LANES
                moved = pltpu.roll(parts[j], turn, 1) if turn else parts[j]
                result = moved if result is None else jnp.where(chunk == j, moved, result)
            rows = slice(side * CAP // 2, (side + 1) * CAP // 2)
            first = (side * CAP + kind) * (OWNERS // 4) + block
            slots_ref[pl.ds(first, CAP // 2, stride=OWNERS // 2), :] = result - means[kind][rows]


def vmem(number):
    return [pl.BlockSpec(memory_space=pltpu.VMEM)] * number


def params(limit=VMEM_LIMIT):
    return pltpu.CompilerParams(vmem_limit_bytes=limit)


def cost(flops, size):
    return pl.CostEstimate(flops=flops, bytes_accessed=size, transcendentals=0)


def along(value, axis_groups):
    return lax.all_to_all(
        value, "acq", split_axis=0, concat_axis=0, tiled=True, axis_index_groups=axis_groups
    )


def exchange_sum(value):
    for axis, steps in (("acq", (1,)), ("strip", (1, 2, 3))):
        size = lax.axis_size(axis)
        moved = [
            lax.ppermute(value, axis, [(i, i ^ step) for i in range(size)]) for step in steps
        ]
        for part in moved:
            value = value + part
    return value


SHAPE = jax.ShapeDtypeStruct
SCALAR = [pl.BlockSpec(memory_space=pltpu.SMEM)]


def pack(slc_stack):
    batch = 2 * PLANE
    return pl.pallas_call(
        pack_kernel,
        out_shape=SHAPE((PLANE, PLANE, LANES, LANES), BF16),
        in_specs=[pl.BlockSpec(memory_space=pl.ANY)],
        out_specs=pl.BlockSpec(memory_space=pl.ANY),
        scratch_shapes=[
            pltpu.VMEM((8, OWNERS, UPPER * LANES), BF16),
            pltpu.VMEM((2, batch * (LANES + 4), LANES), F32),
            pltpu.VMEM((PLANE, PLANE, LANES, LANES), BF16),
            pltpu.SemaphoreType.DMA((OWNERS // batch,)),
            pltpu.SemaphoreType.DMA((OWNERS // batch,)),
        ],
        compiler_params=params(WIDE_LIMIT),
        name="pack",
    )(slc_stack.reshape(8, OWNERS, UPPER * LANES))


def slot_order(mine, date_pairs, pair_owner, pseudo_inverse):
    return pl.pallas_call(
        slot_kernel,
        out_shape=(
            SHAPE((16, SLOTS), F32),
            SHAPE((CAP, DATES), F32),
            SHAPE((CAP, LANES), F32),
            SHAPE((DATES, ENTRIES), BF16),
            SHAPE((DATES, ENTRIES), BF16),
            SHAPE((8 * LANES, TABLE), BF16),
        ),
        in_specs=SCALAR + vmem(3),
        out_specs=tuple(vmem(6)),
        compiler_params=params(),
        name="slot_order",
        cost_estimate=cost(4_000_000_000, 8_000_000),
    )(mine, date_pairs.T, pair_owner.T, pseudo_inverse)


def inner_coherence(cells, table):
    return pl.pallas_call(
        inner_kernel,
        out_shape=(
            SHAPE((PLANE, SPAN // 2 * INNER, LANES), F32),
            SHAPE((2 * SPAN, LANES), F32),
            SHAPE(table.shape, BF16),
        ),
        in_specs=vmem(2),
        out_specs=tuple(vmem(3)),
        scratch_shapes=[
            pltpu.VMEM((4 * TOGETHER, OWN * 8, LANES), F32),
            pltpu.VMEM((PLANE * OWN, 8 * LANES), F32),
            pltpu.VMEM((PLANE * OWN + 8, LANES), F32),
        ],
        compiler_params=params(),
        name="coherence",
        cost_estimate=cost(4_000_000_000, 8_000_000),
    )(cells, table)


def edge_coherence(last, after, before, first, table, inner, inner_sums):
    return pl.pallas_call(
        edge_kernel,
        out_shape=(
            SHAPE((PLANE, SPAN // 2 * OWN, LANES), F32),
            SHAPE((4 * SPAN, LANES), F32),
        ),
        in_specs=vmem(7),
        out_specs=tuple(vmem(2)),
        scratch_shapes=[
            pltpu.VMEM((4 * TOGETHER, 2 * SPAN * 8, LANES), F32),
            pltpu.VMEM((PLANE * 2 * SPAN, 8 * LANES), F32),
            pltpu.VMEM((PLANE * 2 * SPAN + 8, LANES), F32),
        ],
        compiler_params=params(),
        name="edge",
        cost_estimate=cost(2_000_000_000, 4_000_000),
    )(last, after, before, first, table, inner, inner_sums)


def select(mine, coherence, code, sums):
    return pl.pallas_call(
        select_kernel,
        out_shape=SHAPE((OWNERS * ROWS, LANES), F32),
        in_specs=SCALAR + vmem(3),
        out_specs=vmem(1)[0],
        compiler_params=params(),
        name="select",
        cost_estimate=cost(2_000_000_000, 4_000_000),
    )(mine, coherence, code, sums)


def invert(mine, coherence, high, low):
    return pl.pallas_call(
        series_kernel,
        out_shape=SHAPE((2 * LOOKS, DATES), F32),
        in_specs=SCALAR + vmem(3),
        out_specs=vmem(1)[0],
        compiler_params=params(WIDE_LIMIT),
        name="series",
        cost_estimate=cost(1_000_000_000, 3_000_000),
    )(mine, coherence, high, low)


def output(got, high, low, own_early, own_lag, series):
    return pl.pallas_call(
        output_kernel,
        out_shape=(SHAPE((2 * LOOKS, DATES), F32), SHAPE((CAP * 2 * UPPER, LANES), F32)),
        in_specs=vmem(6),
        out_specs=tuple(vmem(2)),
        compiler_params=params(),
        name="referenced",
    )(got, high, low, own_early, own_lag, series)


def on_device(slc_stack, date_pairs, pair_owner, pseudo_inverse):
    size = lax.axis_size("acq")
    planes = [[start + w for w in PLANE_ORDER] for start in range(0, size, PLANE)]
    pillars = [[start + PLANE * z for z in PILLAR_ORDER] for start in range(PLANE)]
    mine = lax.axis_index("acq").astype(jnp.int32).reshape(1)
    cells = along(pack(slc_stack), planes)
    ordered = slot_order(mine, date_pairs, pair_owner, pseudo_inverse)
    cells, ordered = lax.optimization_barrier((cells, ordered))
    code, own_early, own_lag, high, low, table = ordered
    first, last = (
        [cells[PLANE_PLACE[w]:PLANE:PLANE // 2, half:half + HALF] for half in (0, HALF)]
        for w in (0, PLANE - 2)
    )
    after = lax.ppermute(first[0], "acq", [(i, (i - PLANE) % size) for i in range(size)])
    before = lax.ppermute(last[1], "acq", [(i, (i + PLANE) % size) for i in range(size)])
    inner, sums, table = inner_coherence(cells, table)
    parts, sums = edge_coherence(last[0], after, before, first[1], table, inner, sums)
    coherence = along(parts, pillars)
    packed = select(mine, coherence, code, exchange_sum(sums))
    got = lax.all_to_all(
        packed.reshape(OWNERS, 1, ROWS * LANES), "acq", split_axis=0, concat_axis=0, tiled=True
    ).reshape(OWNERS * ROWS, LANES)
    series = invert(mine, coherence, high, low)
    series, slots = output(got, high, low, own_early, own_lag, series)
    return (
        series.reshape(1, 1, 2, LOOKS, DATES),
        slots.reshape(CAP, 2, 1, OWNERS * LOOKS),
    )


def solution(mesh):
    placed = (P("acq", None, "strip", None, None), P(), P(), P())
    return jax.shard_map(
        on_device,
        mesh=mesh,
        in_specs=placed,
        out_specs=(P("strip", "acq", None, None, None), P("acq", None, "strip", None)),
        check_vma=False,
    )
```

```python
import jax
import jax.numpy as jnp
from jax import lax
from jax.experimental import pallas as pl
from jax.experimental.pallas import tpu as pltpu
from jax.sharding import PartitionSpec as P

DATES = 256
PAIRS = 1024
OWNERS = 64
CAP = 32
SLOTS = OWNERS * CAP
SPAN = 8
UPPER = 16
LOOKS = 32
LANES = 128
ENTRIES = SPAN * DATES
PLANE = 8
OWN = 4 * PLANE
INNER = OWN - SPAN
TOGETHER = 8
ROWS = CAP // 2 + 3
HALF = PLANE // 2
PLANE_ORDER = (0, 2, 4, 6, 1, 3, 5, 7)
PLANE_PLACE = tuple(PLANE_ORDER.index(w) for w in range(PLANE))
PILLAR_ORDER = (0, 4, 1, 5, 2, 6, 3, 7)
PILLAR_PLACE = tuple(PILLAR_ORDER.index(z) for z in range(PLANE))
SLOT_ORDER = (0, 4, 1, 5, 2, 6, 3, 7)
SLOT_PLACE = tuple(
    SLOT_ORDER.index(owner // PLANE) * PLANE + owner % PLANE for owner in range(OWNERS)
)
TABLE = (1 + SPAN // 2) * LANES
VMEM_LIMIT = 20 * 1024 * 1024
WIDE_LIMIT = 58 * 1024 * 1024
F32 = jnp.float32
BF16 = jnp.bfloat16


def dot_nt(left, right):
    return lax.dot_general(
        left, right, (((1,), (1,)), ((), ())), preferred_element_type=F32
    )


def dot_nn(left, right):
    return jnp.dot(left, right, preferred_element_type=F32)


def iota(shape, axis):
    return lax.broadcasted_iota(jnp.int32, shape, axis)


def halves(value):
    high = value.astype(BF16)
    return high, (value - high.astype(F32)).astype(BF16)


def flags(mask):
    return mask.astype(F32).astype(BF16)


def skew_rows(band_ref, dates):
    for start in range(0, band_ref.shape[1], LANES):
        value = band_ref[:, start:start + LANES]
        row = iota(value.shape, 0)
        for bit in (1, 2, 4):
            value = jnp.where((row & bit) != 0, pltpu.roll(value, LANES - bit, 1), value)
        parts = []
        for first in range(0, value.shape[0], 8):
            turn = first % dates
            part = value[first:first + 8]
            parts.append(pltpu.roll(part, LANES - turn, 1) if turn else part)
        band_ref[:, start:start + LANES] = jnp.concatenate(parts, axis=0)


def cell_row(date, kind, u):
    return (u // 4) * 32 + date * 8 + (u % 4) * 2 + kind


def pack_kernel(image_ref, sent_ref, held_ref, wide_ref, ready_ref, come_sem, gone_sem):
    batch = 2 * PLANE
    pitch = LANES + 4
    chunks = OWNERS // batch
    coming, going = [], []
    for chunk in range(chunks):
        rows = pl.ds(chunk * batch, batch)
        copy = pltpu.make_async_copy(
            image_ref.at[:, rows, :], held_ref.at[:, rows, :], come_sem.at[chunk]
        )
        copy.start()
        coming.append(copy)
    for chunk in range(chunks):
        coming[chunk].wait()
        rows = slice(chunk * batch, (chunk + 1) * batch)
        for part in range(8):
            for u in range(UPPER):
                row = cell_row(part // 2, part % 2, u)
                wide_ref[chunk % 2, pl.ds(row, batch, stride=pitch), :] = held_ref[
                    part, rows, u * LANES:(u + 1) * LANES
                ].astype(F32)
        for block in range(batch):
            ready_ref[PLANE_PLACE[block % PLANE], 2 * chunk + block // PLANE] = wide_ref[
                chunk % 2, block * pitch:block * pitch + LANES, :
            ].astype(BF16)
        tiles = pl.ds(2 * chunk, 2)
        copy = pltpu.make_async_copy(
            ready_ref.at[:, tiles], sent_ref.at[:, tiles], gone_sem.at[chunk]
        )
        copy.start()
        going.append(copy)
    for copy in going:
        copy.wait()


def slot_kernel(
    mine_ref, dates_ref, owner_ref, pinv_ref,
    code_ref, own_early_ref, own_lag_ref, high_ref, low_ref, table_ref,
):
    owned = iota((OWNERS, PAIRS), 0) == owner_ref[...]
    earlier = flags(iota((PAIRS, PAIRS), 0) < iota((PAIRS, PAIRS), 1))
    before = dot_nn(flags(owned), earlier)
    rank = jnp.sum(jnp.where(owned, before, 0.0), axis=0, keepdims=True)
    slot = owner_ref[...] * CAP + rank.astype(jnp.int32)
    early = dates_ref[0:1, :]
    lag = dates_ref[1:2, :] - early
    entry = (lag - 1) * DATES + early
    numbers = jnp.concatenate(
        [
            jnp.broadcast_to((early + 1).astype(F32), (LANES, PAIRS)),
            jnp.broadcast_to(lag.astype(F32), (LANES, PAIRS)),
        ],
        axis=0,
    ).astype(BF16)
    found = dot_nt(flags(iota((CAP, PAIRS), 0) + mine_ref[0] * CAP == slot), numbers)
    wide = jnp.concatenate([found[:, :LANES], found[:, :LANES]], axis=1)
    own_early_ref[...] = (wide == iota((CAP, DATES), 1).astype(F32) + 1.0).astype(F32)
    own_lag_ref[...] = found[:, LANES:]
    high, low = halves(pinv_ref[...])
    step = 256
    for start in range(0, SLOTS, step):
        rows = slice(start, start + step)
        place = iota((step, PAIRS), 0) + start
        code = dot_nt(numbers, flags(place == slot))
        code_ref[0:8, rows] = code[0:8]
        code_ref[8:16, rows] = code[LANES:LANES + 8]
        chosen = flags(place == entry)
        weight = dot_nt(high, chosen) + dot_nt(low, chosen)
        high_ref[:, rows], low_ref[:, rows] = halves(weight)
    for block in range(8):
        shape = (LANES, TABLE)
        row = iota(shape, 0)
        col = iota(shape, 1)
        inner = row // 16
        look = (block // 2) * 8 + (inner % 4) * 2 + inner // 4
        lag_of = jnp.where(col < LANES, 0, col // (LANES // 2) - 1)
        kind = jnp.where(col < LANES, 0, (col // LOOKS) % 2)
        match = (row % 16 == lag_of) & (col % LOOKS == look) & (kind == block % 2)
        table_ref[block * LANES:(block + 1) * LANES, :] = jnp.where(
            match, 1.0 / 64.0, 0.0
        ).astype(BF16)


def window_masks():
    side_of = (iota((1, 2 * LANES), 1) % 32) // 16
    return [flags(side_of == v) for v in range(2)]


def band_blocks(wide_ref, slot, quarter, dates, keep, store):
    gap = jnp.zeros((LANES // 2 - dates, 2 * LANES), BF16)
    spot = iota((dates, LANES), 1) - (iota((dates, LANES), 0) & -8)
    packed = [None, None]
    for sub in range(4):
        real = wide_ref[slot, pl.ds(2 * sub, dates, stride=8), :]
        imag = wide_ref[slot, pl.ds(2 * sub + 1, dates, stride=8), :]
        straight = jnp.concatenate([real, imag], axis=1).astype(BF16)
        crossed = jnp.concatenate([imag, -real], axis=1).astype(BF16)
        window = jnp.concatenate([straight * keep[0], gap, straight * keep[1], gap], axis=0)
        if sub:
            cut = LANES - 16 * sub
            window = jnp.concatenate([window[cut:], window[:cut]], axis=0)
        gram = dot_nt(jnp.concatenate([straight, crossed], axis=0), window)
        inside = ((spot - 16 * sub) & (LANES // 2 - 1)) < 16
        for kind in range(2):
            part = gram[kind * dates:(kind + 1) * dates]
            packed[kind] = jnp.where(inside, part, packed[kind]) if sub else part
    for kind in range(2):
        store((quarter * 2 + kind) * LANES, packed[kind])


def edge_blocks(wide_ref, slot, quarter, keep, store):
    dates = 2 * SPAN
    straight, crossed = [], []
    for sub in range(4):
        real = wide_ref[slot, pl.ds(2 * sub, dates, stride=8), :]
        imag = wide_ref[slot, pl.ds(2 * sub + 1, dates, stride=8), :]
        straight.append(jnp.concatenate([real, imag], axis=1).astype(BF16))
        crossed.append(jnp.concatenate([imag, -real], axis=1).astype(BF16))
    whole = jnp.concatenate(straight, axis=0)
    window = jnp.concatenate([whole * keep[0], whole * keep[1]], axis=0)
    gram = dot_nt(jnp.concatenate([whole] + crossed, axis=0), window)
    sub_of = (iota((dates, LANES), 1) // 16) % 4
    for kind in range(2):
        value = None
        for sub in range(4):
            start = (kind * 4 + sub) * dates
            part = gram[start:start + dates]
            value = part if value is None else jnp.where(sub_of == sub, part, value)
        store((quarter * 2 + kind) * LANES, value)


def normalised(band_ref, table_ref, scale_ref):
    count = band_ref.shape[0]
    high, low = halves(band_ref[...])
    table = dot_nn(high, table_ref[...]) + dot_nn(low, table_ref[...])
    scale = lax.rsqrt(table[:, :LANES] + 1e-06)
    scale_ref[0:count, :] = scale
    scale_ref[count:count + 8, :] = jnp.zeros((8, LANES), F32)
    left = iota((count, LANES), 1) < LANES // 2
    for pair in range(SPAN // 2):
        lag = 2 * pair + 1
        late = jnp.where(left, scale_ref[lag:lag + count, :], scale_ref[lag + 1:lag + 1 + count, :])
        yield pair, table[:, (pair + 1) * LANES:(pair + 2) * LANES] * scale * late


def window_sums(total):
    pick = flags(iota((8, LANES), 1) // LOOKS == iota((8, LANES), 0))
    high, low = halves(jnp.concatenate([total] * (LANES // total.shape[0]), axis=0))
    return (dot_nt(pick, high) + dot_nt(pick, low))[0:4]


def each_tile(tile):
    def body(index, carry):
        for part in range(TOGETHER):
            tile(index * TOGETHER + part, 4 * part)
        return carry

    lax.fori_loop(0, PLANE // TOGETHER, body, 0)


def inner_kernel(
    cells_ref, table_ref, out_ref, sum_ref, table_copy_ref, wide_ref, band_ref, scale_ref
):
    keep = window_masks()

    def tile(index, slot):
        for quarter in range(4):
            rows = slice(quarter * 32, (quarter + 1) * 32)
            for w in range(PLANE):
                wide_ref[slot + quarter, w * 32:(w + 1) * 32] = cells_ref[
                    PLANE_PLACE[w], index, rows, :
                ].astype(F32)

            def store(start, value):
                place = pl.ds(pl.multiple_of(index * OWN, OWN), OWN)
                band_ref[place, start:start + LANES] = value

            band_blocks(wide_ref, slot + quarter, quarter, OWN, keep, store)

    each_tile(tile)
    skew_rows(band_ref, OWN)
    table_copy_ref[...] = table_ref[...]
    rest = jnp.zeros((SPAN, LANES), F32)
    for pair, value in normalised(band_ref, table_ref, scale_ref):
        total = jnp.zeros((INNER, LANES), F32)
        for index in range(PLANE):
            part = value[index * OWN:index * OWN + INNER]
            out_ref[PILLAR_PLACE[index], pair * INNER:(pair + 1) * INNER, :] = part
            total = total + part
        sum_ref[4 * pair:4 * pair + 4, :] = window_sums(jnp.concatenate([total, rest], axis=0))


def edge_kernel(
    last_ref, next_ref, before_ref, first_ref, table_ref, inner_ref, inner_sum_ref,
    out_ref, sum_ref, wide_ref, band_ref, scale_ref,
):
    keep = window_masks()
    count = 2 * SPAN
    for index in range(PLANE):
        early_ref, late_ref = (last_ref, next_ref) if index < HALF else (before_ref, first_ref)
        for quarter in range(4):
            slot = 4 * index + quarter
            rows = slice(quarter * 32, (quarter + 1) * 32)
            for part, source in enumerate((early_ref, late_ref)):
                wide_ref[slot, part * SPAN * 8:(part + 1) * SPAN * 8] = (
                    source[:, index % HALF, rows, :].astype(F32).reshape(SPAN * 8, LANES)
                )

            def store(start, value):
                band_ref[index * count:(index + 1) * count, start:start + LANES] = value

            edge_blocks(wide_ref, slot, quarter, keep, store)
    skew_rows(band_ref, count)
    rest = jnp.zeros((INNER, LANES), F32)
    for pair, value in normalised(band_ref, table_ref, scale_ref):
        totals = [jnp.zeros((SPAN, LANES), F32), jnp.zeros((SPAN, LANES), F32)]
        for index in range(PLANE):
            part = value[index * count:index * count + SPAN]
            out_ref[PILLAR_PLACE[index], pair * OWN + INNER:(pair + 1) * OWN, :] = part
            totals[index // HALF] = totals[index // HALF] + part
        out_ref[:, pair * OWN:pair * OWN + INNER, :] = inner_ref[
            :, pair * INNER:(pair + 1) * INNER, :
        ]
        rows = slice(4 * pair, 4 * pair + 4)
        sums = window_sums(jnp.concatenate([rest, totals[0]], axis=0))
        sum_ref[rows, :] = inner_sum_ref[rows, :] + sums
        sum_ref[2 * SPAN + 4 * pair:2 * SPAN + 4 * pair + 4, :] = window_sums(totals[1])


def split_table(mine_ref, table_ref):
    upper = mine_ref[0] // PLANE >= HALF
    left = iota((DATES, LANES), 1) < LANES // 2
    columns = []
    for pair in range(SPAN // 2):
        inner = slice(pair * OWN, pair * OWN + INNER)
        edge = slice(pair * OWN + INNER, (pair + 1) * OWN)
        parts = []
        for plane in range(PLANE):
            parts.append(table_ref[PILLAR_PLACE[plane], inner, :])
            same = table_ref[PILLAR_PLACE[plane], edge, :]
            after = table_ref[PILLAR_PLACE[(plane + 1) % PLANE], edge, :]
            parts.append(jnp.where(upper, after, same))
        value = jnp.concatenate(parts, axis=0)
        top = value.astype(BF16).astype(F32)
        rest = pltpu.roll(value - top, LANES // 2, 1)
        columns.append(jnp.where(left, top, rest).astype(BF16))
        columns.append(jnp.where(left, rest, top).astype(BF16))
    return columns


def select_kernel(mine_ref, table_ref, code_ref, sum_ref, send_ref):
    coherence = jnp.concatenate(split_table(mine_ref, table_ref), axis=1)
    row = iota((2 * SPAN, LANES), 0) - SPAN * (mine_ref[0] % 2)
    extra = []
    for part in range(2):
        wanted = row == 4 * part + iota((2 * SPAN, LANES), 1) // OWN
        extra.append(jnp.sum(jnp.where(wanted, sum_ref[0:2 * SPAN], 0.0), axis=0, keepdims=True))
    wanted = row == iota((2 * SPAN, LANES), 1) // SPAN
    extra.append(jnp.sum(jnp.where(wanted, sum_ref[2 * SPAN:], 0.0), axis=0, keepdims=True))
    extra = jnp.concatenate(extra, axis=0)
    step = 256
    half = iota((CAP // 2, LANES), 1) < LANES // 2
    column = iota((step, DATES), 1).astype(F32) + 1.0
    for start in range(0, SLOTS, step):
        rows = slice(start, start + step)
        early = jnp.broadcast_to(code_ref[0:1, rows], (LANES, step)).T
        lag_of = jnp.broadcast_to(code_ref[8:9, rows], (LANES, step)).T
        onehot = flags(jnp.concatenate([early, early], axis=1) == column)
        found = dot_nn(onehot, coherence)
        value = jnp.zeros((step, LANES), F32)
        for lag in range(1, SPAN + 1):
            value = jnp.where(lag_of == float(lag), found[:, (lag - 1) * LANES:lag * LANES], value)
        value = value + pltpu.roll(value, LANES // 2, 1)
        for part in range(step // CAP):
            first = part * CAP
            middle = first + CAP // 2
            target = SLOT_PLACE[start // CAP + part] * ROWS
            send_ref[target:target + CAP // 2, :] = jnp.where(
                half, value[first:middle], value[middle:first + CAP]
            )
            send_ref[target + CAP // 2:target + ROWS, :] = extra


def series_kernel(mine_ref, table_ref, high_ref, low_ref, series_ref):
    columns = split_table(mine_ref, table_ref)
    series = jnp.zeros((DATES, LANES), F32)
    for lag in range(SPAN):
        rows = slice(lag * DATES, (lag + 1) * DATES)
        series = series + dot_nn(high_ref[:, rows], columns[lag])
        series = series + dot_nn(low_ref[:, rows], columns[lag])
    series = series + pltpu.roll(series, LANES // 2, 1)
    series_ref[...] = series.T[0:LANES // 2]


def output_kernel(
    got_ref, high_ref, low_ref, own_early_ref, own_lag_ref, series_in_ref, series_ref, slots_ref
):
    group = iota((PLANE, LANES), 1) // OWN
    placed = {}
    for part in range(2):
        sums = got_ref[pl.ds(CAP // 2 + part, OWNERS, stride=ROWS), :] * (1.0 / 8192.0)
        for plane in range(PLANE):
            start = SLOT_PLACE[plane * PLANE]
            value = sums[start:start + PLANE]
            value = value + pltpu.roll(value, 4, 0)
            value = value + pltpu.roll(value, 2, 0)
            for j in range(4):
                turn = (OWN * (plane - j)) % LANES
                moved = pltpu.roll(value, turn, 1) if turn else value
                key = part, j, plane // 4
                placed[key] = jnp.where(group == plane % 4, moved, placed[key]) if key in placed else moved
    group = iota((PLANE, LANES), 1) // SPAN
    sums = got_ref[pl.ds(CAP // 2 + 2, OWNERS, stride=ROWS), :] * (1.0 / 8192.0)
    for plane in range(PLANE):
        start = SLOT_PLACE[plane * PLANE]
        value = sums[start:start + PLANE]
        value = value + pltpu.roll(value, 4, 0)
        value = value + pltpu.roll(value, 2, 0)
        target = (plane - 1) % PLANE
        spot = (target % 4) * 4 + 3
        for row in range(SPAN):
            turn = SPAN * (spot - row) % LANES
            moved = pltpu.roll(value, turn, 1) if turn else value
            key = row // 4, row % 4, target // 4
            placed[key] = placed[key] + jnp.where(group == spot, moved, 0.0)
    rows = [
        jnp.concatenate([placed[part, j, 0], placed[part, j, 1]], axis=1)[core:core + 1]
        for core in range(2) for part in range(2) for j in range(4)
    ]
    total = jnp.concatenate(rows, axis=0)
    high, low = halves(total)
    lag_of = own_lag_ref[:, 0:1]
    shift = [jnp.zeros((1, DATES), F32) for _ in range(2)]
    found = [jnp.zeros((CAP, DATES), F32) for _ in range(2)]
    for lag in range(SPAN):
        rows = slice(lag * DATES, (lag + 1) * DATES)
        part = (
            dot_nt(high, high_ref[:, rows])
            + dot_nt(low, high_ref[:, rows])
            + dot_nt(high, low_ref[:, rows])
        )
        for kind in range(2):
            row = 2 * lag + kind
            shift[kind] = shift[kind] + part[row:row + 1]
            found[kind] = jnp.where(lag_of == float(lag + 1), total[row:row + 1], found[kind])
    means = []
    for kind in range(2):
        rows = slice(kind * LOOKS, (kind + 1) * LOOKS)
        series_ref[rows, :] = series_in_ref[rows, :] - shift[kind]
        means.append(jnp.sum(found[kind] * own_early_ref[...], axis=1, keepdims=True))
    chunk = iota((CAP // 2, LANES), 1) // LOOKS
    for block in range(OWNERS // 4):
        starts = [SLOT_PLACE[4 * block + j] * ROWS for j in range(4)]
        parts = [got_ref[start:start + CAP // 2, :] for start in starts]
        for t in range(4):
            side, kind = t // 2, t % 2
            result = None
            for j in range(4):
                turn = (LOOKS * (j - t)) % LANES
                moved = pltpu.roll(parts[j], turn, 1) if turn else parts[j]
                result = moved if result is None else jnp.where(chunk == j, moved, result)
            rows = slice(side * CAP // 2, (side + 1) * CAP // 2)
            first = (side * CAP + kind) * (OWNERS // 4) + block
            slots_ref[pl.ds(first, CAP // 2, stride=OWNERS // 2), :] = result - means[kind][rows]


def vmem(number):
    return [pl.BlockSpec(memory_space=pltpu.VMEM)] * number


def params(limit=VMEM_LIMIT):
    return pltpu.CompilerParams(vmem_limit_bytes=limit)


def cost(flops, size):
    return pl.CostEstimate(flops=flops, bytes_accessed=size, transcendentals=0)


def along(value, axis_groups):
    return lax.all_to_all(
        value, "acq", split_axis=0, concat_axis=0, tiled=True, axis_index_groups=axis_groups
    )


def exchange_sum(value):
    for axis, steps in (("acq", (1,)), ("strip", (1, 2, 3))):
        size = lax.axis_size(axis)
        moved = [
            lax.ppermute(value, axis, [(i, i ^ step) for i in range(size)]) for step in steps
        ]
        for part in moved:
            value = value + part
    return value


SHAPE = jax.ShapeDtypeStruct
SCALAR = [pl.BlockSpec(memory_space=pltpu.SMEM)]


def pack(slc_stack):
    batch = 2 * PLANE
    return pl.pallas_call(
        pack_kernel,
        out_shape=SHAPE((PLANE, PLANE, LANES, LANES), BF16),
        in_specs=[pl.BlockSpec(memory_space=pl.ANY)],
        out_specs=pl.BlockSpec(memory_space=pl.ANY),
        scratch_shapes=[
            pltpu.VMEM((8, OWNERS, UPPER * LANES), BF16),
            pltpu.VMEM((2, batch * (LANES + 4), LANES), F32),
            pltpu.VMEM((PLANE, PLANE, LANES, LANES), BF16),
            pltpu.SemaphoreType.DMA((OWNERS // batch,)),
            pltpu.SemaphoreType.DMA((OWNERS // batch,)),
        ],
        compiler_params=params(WIDE_LIMIT),
        name="pack",
    )(slc_stack.reshape(8, OWNERS, UPPER * LANES))


def slot_order(mine, date_pairs, pair_owner, pseudo_inverse):
    return pl.pallas_call(
        slot_kernel,
        out_shape=(
            SHAPE((16, SLOTS), F32),
            SHAPE((CAP, DATES), F32),
            SHAPE((CAP, LANES), F32),
            SHAPE((DATES, ENTRIES), BF16),
            SHAPE((DATES, ENTRIES), BF16),
            SHAPE((8 * LANES, TABLE), BF16),
        ),
        in_specs=SCALAR + vmem(3),
        out_specs=tuple(vmem(6)),
        compiler_params=params(),
        name="slot_order",
        cost_estimate=cost(4_000_000_000, 8_000_000),
    )(mine, date_pairs.T, pair_owner.T, pseudo_inverse)


def inner_coherence(cells, table):
    return pl.pallas_call(
        inner_kernel,
        out_shape=(
            SHAPE((PLANE, SPAN // 2 * INNER, LANES), F32),
            SHAPE((2 * SPAN, LANES), F32),
            SHAPE(table.shape, BF16),
        ),
        in_specs=vmem(2),
        out_specs=tuple(vmem(3)),
        scratch_shapes=[
            pltpu.VMEM((4 * TOGETHER, OWN * 8, LANES), F32),
            pltpu.VMEM((PLANE * OWN, 8 * LANES), F32),
            pltpu.VMEM((PLANE * OWN + 8, LANES), F32),
        ],
        compiler_params=params(),
        name="coherence",
        cost_estimate=cost(4_000_000_000, 8_000_000),
    )(cells, table)


def edge_coherence(last, after, before, first, table, inner, inner_sums):
    return pl.pallas_call(
        edge_kernel,
        out_shape=(
            SHAPE((PLANE, SPAN // 2 * OWN, LANES), F32),
            SHAPE((4 * SPAN, LANES), F32),
        ),
        in_specs=vmem(7),
        out_specs=tuple(vmem(2)),
        scratch_shapes=[
            pltpu.VMEM((4 * TOGETHER, 2 * SPAN * 8, LANES), F32),
            pltpu.VMEM((PLANE * 2 * SPAN, 8 * LANES), F32),
            pltpu.VMEM((PLANE * 2 * SPAN + 8, LANES), F32),
        ],
        compiler_params=params(),
        name="edge",
        cost_estimate=cost(2_000_000_000, 4_000_000),
    )(last, after, before, first, table, inner, inner_sums)


def select(mine, coherence, code, sums):
    return pl.pallas_call(
        select_kernel,
        out_shape=SHAPE((OWNERS * ROWS, LANES), F32),
        in_specs=SCALAR + vmem(3),
        out_specs=vmem(1)[0],
        compiler_params=params(),
        name="select",
        cost_estimate=cost(2_000_000_000, 4_000_000),
    )(mine, coherence, code, sums)


def invert(mine, coherence, high, low):
    return pl.pallas_call(
        series_kernel,
        out_shape=SHAPE((2 * LOOKS, DATES), F32),
        in_specs=SCALAR + vmem(3),
        out_specs=vmem(1)[0],
        compiler_params=params(WIDE_LIMIT),
        name="series",
        cost_estimate=cost(1_000_000_000, 3_000_000),
    )(mine, coherence, high, low)


def output(got, high, low, own_early, own_lag, series):
    return pl.pallas_call(
        output_kernel,
        out_shape=(SHAPE((2 * LOOKS, DATES), F32), SHAPE((CAP * 2 * UPPER, LANES), F32)),
        in_specs=vmem(6),
        out_specs=tuple(vmem(2)),
        compiler_params=params(),
        name="referenced",
    )(got, high, low, own_early, own_lag, series)


def on_device(slc_stack, date_pairs, pair_owner, pseudo_inverse):
    size = lax.axis_size("acq")
    planes = [[start + w for w in PLANE_ORDER] for start in range(0, size, PLANE)]
    pillars = [[start + PLANE * z for z in PILLAR_ORDER] for start in range(PLANE)]
    mine = lax.axis_index("acq").astype(jnp.int32).reshape(1)
    cells = along(pack(slc_stack), planes)
    ordered = slot_order(mine, date_pairs, pair_owner, pseudo_inverse)
    cells, ordered = lax.optimization_barrier((cells, ordered))
    code, own_early, own_lag, high, low, table = ordered
    first, last = (
        [cells[PLANE_PLACE[w]:PLANE:PLANE // 2, half:half + HALF] for half in (0, HALF)]
        for w in (0, PLANE - 2)
    )
    after = lax.ppermute(first[0], "acq", [(i, (i - PLANE) % size) for i in range(size)])
    before = lax.ppermute(last[1], "acq", [(i, (i + PLANE) % size) for i in range(size)])
    inner, sums, table = inner_coherence(cells, table)
    parts, sums = edge_coherence(last[0], after, before, first[1], table, inner, sums)
    coherence = along(parts, pillars)
    packed = select(mine, coherence, code, exchange_sum(sums))
    everyone = [[PLANE * z + w for z in SLOT_ORDER for w in range(PLANE)]]
    got = along(packed.reshape(OWNERS, 1, ROWS * LANES), everyone).reshape(OWNERS * ROWS, LANES)
    series = invert(mine, coherence, high, low)
    series, slots = output(got, high, low, own_early, own_lag, series)
    return (
        series.reshape(1, 1, 2, LOOKS, DATES),
        slots.reshape(CAP, 2, 1, OWNERS * LOOKS),
    )


def solution(mesh):
    placed = (P("acq", None, "strip", None, None), P(), P(), P())
    return jax.shard_map(
        on_device,
        mesh=mesh,
        in_specs=placed,
        out_specs=(P("strip", "acq", None, None, None), P("acq", None, "strip", None)),
        check_vma=False,
    )
```

```python
import jax
import jax.numpy as jnp
from jax import lax
from jax.experimental import pallas as pl
from jax.experimental.pallas import tpu as pltpu
from jax.sharding import PartitionSpec as P

DATES = 256
PAIRS = 1024
OWNERS = 64
CAP = 32
SLOTS = OWNERS * CAP
SPAN = 8
UPPER = 16
LOOKS = 32
LANES = 128
ENTRIES = SPAN * DATES
PLANE = 8
OWN = 4 * PLANE
INNER = OWN - SPAN
TOGETHER = 8
ROWS = CAP // 2 + 3
HALF = PLANE // 2
PLANE_ORDER = (0, 2, 4, 6, 1, 3, 5, 7)
PLANE_PLACE = tuple(PLANE_ORDER.index(w) for w in range(PLANE))
PILLAR_ORDER = (0, 4, 1, 5, 2, 6, 3, 7)
PILLAR_PLACE = tuple(PILLAR_ORDER.index(z) for z in range(PLANE))
SLOT_ORDER = (0, 4, 1, 5, 2, 6, 3, 7)
SLOT_PLACE = tuple(
    SLOT_ORDER.index(owner // PLANE) * PLANE + owner % PLANE for owner in range(OWNERS)
)
TABLE = (1 + SPAN // 2) * LANES
VMEM_LIMIT = 50 * 1024 * 1024
WIDE_LIMIT = 58 * 1024 * 1024
F32 = jnp.float32
BF16 = jnp.bfloat16


def dot_nt(left, right):
    return lax.dot_general(
        left, right, (((1,), (1,)), ((), ())), preferred_element_type=F32
    )


def dot_nn(left, right):
    return jnp.dot(left, right, preferred_element_type=F32)


def iota(shape, axis):
    return lax.broadcasted_iota(jnp.int32, shape, axis)


def halves(value):
    high = value.astype(BF16)
    return high, (value - high.astype(F32)).astype(BF16)


def flags(mask):
    return mask.astype(F32).astype(BF16)


def skew_rows(band_ref, dates):
    for start in range(0, band_ref.shape[1], LANES):
        value = band_ref[:, start:start + LANES]
        row = iota(value.shape, 0)
        for bit in (1, 2, 4):
            value = jnp.where((row & bit) != 0, pltpu.roll(value, LANES - bit, 1), value)
        parts = []
        for first in range(0, value.shape[0], 8):
            turn = first % dates
            part = value[first:first + 8]
            parts.append(pltpu.roll(part, LANES - turn, 1) if turn else part)
        band_ref[:, start:start + LANES] = jnp.concatenate(parts, axis=0)


def cell_row(date, kind, u):
    return (u // 4) * 32 + date * 8 + (u % 4) * 2 + kind


def pack_kernel(image_ref, sent_ref, held_ref, wide_ref, ready_ref, come_sem, gone_sem):
    batch = 2 * PLANE
    pitch = LANES + 4
    chunks = OWNERS // batch
    coming, going = [], []
    for chunk in range(chunks):
        rows = pl.ds(chunk * batch, batch)
        copy = pltpu.make_async_copy(
            image_ref.at[:, rows, :], held_ref.at[:, rows, :], come_sem.at[chunk]
        )
        copy.start()
        coming.append(copy)
    for chunk in range(chunks):
        coming[chunk].wait()
        rows = slice(chunk * batch, (chunk + 1) * batch)
        for part in range(8):
            for u in range(UPPER):
                row = cell_row(part // 2, part % 2, u)
                wide_ref[chunk % 2, pl.ds(row, batch, stride=pitch), :] = held_ref[
                    part, rows, u * LANES:(u + 1) * LANES
                ].astype(F32)
        for block in range(batch):
            ready_ref[PLANE_PLACE[block % PLANE], 2 * chunk + block // PLANE] = wide_ref[
                chunk % 2, block * pitch:block * pitch + LANES, :
            ].astype(BF16)
        tiles = pl.ds(2 * chunk, 2)
        copy = pltpu.make_async_copy(
            ready_ref.at[:, tiles], sent_ref.at[:, tiles], gone_sem.at[chunk]
        )
        copy.start()
        going.append(copy)
    for copy in going:
        copy.wait()


def slot_kernel(
    mine_ref, dates_ref, owner_ref, pinv_ref,
    code_ref, own_early_ref, own_lag_ref, high_ref, low_ref, table_ref,
):
    owned = iota((OWNERS, PAIRS), 0) == owner_ref[...]
    earlier = flags(iota((PAIRS, PAIRS), 0) < iota((PAIRS, PAIRS), 1))
    before = dot_nn(flags(owned), earlier)
    rank = jnp.sum(jnp.where(owned, before, 0.0), axis=0, keepdims=True)
    slot = owner_ref[...] * CAP + rank.astype(jnp.int32)
    early = dates_ref[0:1, :]
    lag = dates_ref[1:2, :] - early
    entry = (lag - 1) * DATES + early
    numbers = jnp.concatenate(
        [
            jnp.broadcast_to((early + 1).astype(F32), (LANES, PAIRS)),
            jnp.broadcast_to(lag.astype(F32), (LANES, PAIRS)),
        ],
        axis=0,
    ).astype(BF16)
    found = dot_nt(flags(iota((CAP, PAIRS), 0) + mine_ref[0] * CAP == slot), numbers)
    wide = jnp.concatenate([found[:, :LANES], found[:, :LANES]], axis=1)
    own_early_ref[...] = (wide == iota((CAP, DATES), 1).astype(F32) + 1.0).astype(F32)
    own_lag_ref[...] = found[:, LANES:]
    high, low = halves(pinv_ref[...])
    step = 256
    for start in range(0, SLOTS, step):
        rows = slice(start, start + step)
        place = iota((step, PAIRS), 0) + start
        code = dot_nt(numbers, flags(place == slot))
        code_ref[0:8, rows] = code[0:8]
        code_ref[8:16, rows] = code[LANES:LANES + 8]
        chosen = flags(place == entry)
        weight = dot_nt(high, chosen) + dot_nt(low, chosen)
        high_ref[:, rows], low_ref[:, rows] = halves(weight)
    for block in range(8):
        shape = (LANES, TABLE)
        row = iota(shape, 0)
        col = iota(shape, 1)
        inner = row // 16
        look = (block // 2) * 8 + (inner % 4) * 2 + inner // 4
        lag_of = jnp.where(col < LANES, 0, col // (LANES // 2) - 1)
        kind = jnp.where(col < LANES, 0, (col // LOOKS) % 2)
        match = (row % 16 == lag_of) & (col % LOOKS == look) & (kind == block % 2)
        table_ref[block * LANES:(block + 1) * LANES, :] = jnp.where(
            match, 1.0 / 64.0, 0.0
        ).astype(BF16)


def window_masks():
    side_of = (iota((1, 2 * LANES), 1) % 32) // 16
    return [flags(side_of == v) for v in range(2)]


def band_blocks(wide_ref, slot, quarter, dates, keep, store):
    gap = jnp.zeros((LANES // 2 - dates, 2 * LANES), BF16)
    spot = iota((dates, LANES), 1) - (iota((dates, LANES), 0) & -8)
    packed = [None, None]
    for sub in range(4):
        real = wide_ref[slot, pl.ds(2 * sub, dates, stride=8), :]
        imag = wide_ref[slot, pl.ds(2 * sub + 1, dates, stride=8), :]
        straight = jnp.concatenate([real, imag], axis=1).astype(BF16)
        crossed = jnp.concatenate([imag, -real], axis=1).astype(BF16)
        window = jnp.concatenate([straight * keep[0], gap, straight * keep[1], gap], axis=0)
        if sub:
            cut = LANES - 16 * sub
            window = jnp.concatenate([window[cut:], window[:cut]], axis=0)
        gram = dot_nt(jnp.concatenate([straight, crossed], axis=0), window)
        inside = ((spot - 16 * sub) & (LANES // 2 - 1)) < 16
        for kind in range(2):
            part = gram[kind * dates:(kind + 1) * dates]
            packed[kind] = jnp.where(inside, part, packed[kind]) if sub else part
    for kind in range(2):
        store((quarter * 2 + kind) * LANES, packed[kind])


def edge_blocks(wide_ref, slot, quarter, keep, store):
    dates = 2 * SPAN
    straight, crossed = [], []
    for sub in range(4):
        real = wide_ref[slot, pl.ds(2 * sub, dates, stride=8), :]
        imag = wide_ref[slot, pl.ds(2 * sub + 1, dates, stride=8), :]
        straight.append(jnp.concatenate([real, imag], axis=1).astype(BF16))
        crossed.append(jnp.concatenate([imag, -real], axis=1).astype(BF16))
    whole = jnp.concatenate(straight, axis=0)
    window = jnp.concatenate([whole * keep[0], whole * keep[1]], axis=0)
    gram = dot_nt(jnp.concatenate([whole] + crossed, axis=0), window)
    sub_of = (iota((dates, LANES), 1) // 16) % 4
    for kind in range(2):
        value = None
        for sub in range(4):
            start = (kind * 4 + sub) * dates
            part = gram[start:start + dates]
            value = part if value is None else jnp.where(sub_of == sub, part, value)
        store((quarter * 2 + kind) * LANES, value)


def normalised(band_ref, table_ref, scale_ref):
    count = band_ref.shape[0]
    high, low = halves(band_ref[...])
    table = dot_nn(high, table_ref[...]) + dot_nn(low, table_ref[...])
    scale = lax.rsqrt(table[:, :LANES] + 1e-06)
    scale_ref[0:count, :] = scale
    scale_ref[count:count + 8, :] = jnp.zeros((8, LANES), F32)
    left = iota((count, LANES), 1) < LANES // 2
    for pair in range(SPAN // 2):
        lag = 2 * pair + 1
        late = jnp.where(left, scale_ref[lag:lag + count, :], scale_ref[lag + 1:lag + 1 + count, :])
        yield pair, table[:, (pair + 1) * LANES:(pair + 2) * LANES] * scale * late


def window_sums(total):
    pick = flags(iota((8, LANES), 1) // LOOKS == iota((8, LANES), 0))
    high, low = halves(jnp.concatenate([total] * (LANES // total.shape[0]), axis=0))
    return (dot_nt(pick, high) + dot_nt(pick, low))[0:4]


def each_tile(tile):
    def body(index, carry):
        for part in range(TOGETHER):
            tile(index * TOGETHER + part, 4 * part)
        return carry

    lax.fori_loop(0, PLANE // TOGETHER, body, 0)


def inner_kernel(
    cells_ref, table_ref, out_ref, sum_ref, table_copy_ref, wide_ref, band_ref, scale_ref
):
    keep = window_masks()

    def tile(index, slot):
        for quarter in range(4):
            rows = slice(quarter * 32, (quarter + 1) * 32)
            for w in range(PLANE):
                wide_ref[slot + quarter, w * 32:(w + 1) * 32] = cells_ref[
                    PLANE_PLACE[w], index, rows, :
                ].astype(F32)

            def store(start, value):
                place = pl.ds(pl.multiple_of(index * OWN, OWN), OWN)
                band_ref[place, start:start + LANES] = value

            band_blocks(wide_ref, slot + quarter, quarter, OWN, keep, store)

    each_tile(tile)
    skew_rows(band_ref, OWN)
    table_copy_ref[...] = table_ref[...]
    rest = jnp.zeros((SPAN, LANES), F32)
    for pair, value in normalised(band_ref, table_ref, scale_ref):
        total = jnp.zeros((INNER, LANES), F32)
        for index in range(PLANE):
            part = value[index * OWN:index * OWN + INNER]
            out_ref[PILLAR_PLACE[index], pair * INNER:(pair + 1) * INNER, :] = part
            total = total + part
        sum_ref[4 * pair:4 * pair + 4, :] = window_sums(jnp.concatenate([total, rest], axis=0))


def edge_kernel(
    last_ref, next_ref, before_ref, first_ref, table_ref, inner_ref, inner_sum_ref,
    out_ref, sum_ref, wide_ref, band_ref, scale_ref,
):
    keep = window_masks()
    count = 2 * SPAN
    for index in range(PLANE):
        early_ref, late_ref = (last_ref, next_ref) if index < HALF else (before_ref, first_ref)
        for quarter in range(4):
            slot = 4 * index + quarter
            rows = slice(quarter * 32, (quarter + 1) * 32)
            for part, source in enumerate((early_ref, late_ref)):
                wide_ref[slot, part * SPAN * 8:(part + 1) * SPAN * 8] = (
                    source[:, index % HALF, rows, :].astype(F32).reshape(SPAN * 8, LANES)
                )

            def store(start, value):
                band_ref[index * count:(index + 1) * count, start:start + LANES] = value

            edge_blocks(wide_ref, slot, quarter, keep, store)
    skew_rows(band_ref, count)
    rest = jnp.zeros((INNER, LANES), F32)
    for pair, value in normalised(band_ref, table_ref, scale_ref):
        totals = [jnp.zeros((SPAN, LANES), F32), jnp.zeros((SPAN, LANES), F32)]
        for index in range(PLANE):
            part = value[index * count:index * count + SPAN]
            out_ref[PILLAR_PLACE[index], pair * OWN + INNER:(pair + 1) * OWN, :] = part
            totals[index // HALF] = totals[index // HALF] + part
        out_ref[:, pair * OWN:pair * OWN + INNER, :] = inner_ref[
            :, pair * INNER:(pair + 1) * INNER, :
        ]
        rows = slice(4 * pair, 4 * pair + 4)
        sums = window_sums(jnp.concatenate([rest, totals[0]], axis=0))
        sum_ref[rows, :] = inner_sum_ref[rows, :] + sums
        sum_ref[2 * SPAN + 4 * pair:2 * SPAN + 4 * pair + 4, :] = window_sums(totals[1])


def split_table(mine_ref, table_ref):
    upper = mine_ref[0] // PLANE >= HALF
    left = iota((DATES, LANES), 1) < LANES // 2
    columns = []
    for pair in range(SPAN // 2):
        inner = slice(pair * OWN, pair * OWN + INNER)
        edge = slice(pair * OWN + INNER, (pair + 1) * OWN)
        parts = []
        for plane in range(PLANE):
            parts.append(table_ref[PILLAR_PLACE[plane], inner, :])
            same = table_ref[PILLAR_PLACE[plane], edge, :]
            after = table_ref[PILLAR_PLACE[(plane + 1) % PLANE], edge, :]
            parts.append(jnp.where(upper, after, same))
        value = jnp.concatenate(parts, axis=0)
        top = value.astype(BF16).astype(F32)
        rest = pltpu.roll(value - top, LANES // 2, 1)
        columns.append(jnp.where(left, top, rest).astype(BF16))
        columns.append(jnp.where(left, rest, top).astype(BF16))
    return columns


def select_kernel(mine_ref, table_ref, code_ref, sum_ref, send_ref):
    coherence = jnp.concatenate(split_table(mine_ref, table_ref), axis=1)
    row = iota((2 * SPAN, LANES), 0) - SPAN * (mine_ref[0] % 2)
    extra = []
    for part in range(2):
        wanted = row == 4 * part + iota((2 * SPAN, LANES), 1) // OWN
        extra.append(jnp.sum(jnp.where(wanted, sum_ref[0:2 * SPAN], 0.0), axis=0, keepdims=True))
    wanted = row == iota((2 * SPAN, LANES), 1) // SPAN
    extra.append(jnp.sum(jnp.where(wanted, sum_ref[2 * SPAN:], 0.0), axis=0, keepdims=True))
    extra = jnp.concatenate(extra, axis=0)
    step = 256
    half = iota((CAP // 2, LANES), 1) < LANES // 2
    column = iota((step, DATES), 1).astype(F32) + 1.0
    for start in range(0, SLOTS, step):
        rows = slice(start, start + step)
        early = jnp.broadcast_to(code_ref[0:1, rows], (LANES, step)).T
        lag_of = jnp.broadcast_to(code_ref[8:9, rows], (LANES, step)).T
        onehot = flags(jnp.concatenate([early, early], axis=1) == column)
        found = dot_nn(onehot, coherence)
        value = jnp.zeros((step, LANES), F32)
        for lag in range(1, SPAN + 1):
            value = jnp.where(lag_of == float(lag), found[:, (lag - 1) * LANES:lag * LANES], value)
        value = value + pltpu.roll(value, LANES // 2, 1)
        for part in range(step // CAP):
            first = part * CAP
            middle = first + CAP // 2
            target = SLOT_PLACE[start // CAP + part] * ROWS
            send_ref[target:target + CAP // 2, :] = jnp.where(
                half, value[first:middle], value[middle:first + CAP]
            )
            send_ref[target + CAP // 2:target + ROWS, :] = extra


def series_kernel(mine_ref, table_ref, high_ref, low_ref, series_ref):
    columns = split_table(mine_ref, table_ref)
    series = jnp.zeros((DATES, LANES), F32)
    for lag in range(SPAN):
        rows = slice(lag * DATES, (lag + 1) * DATES)
        series = series + dot_nn(high_ref[:, rows], columns[lag])
        series = series + dot_nn(low_ref[:, rows], columns[lag])
    series = series + pltpu.roll(series, LANES // 2, 1)
    series_ref[...] = series.T[0:LANES // 2]


def output_kernel(
    got_ref, high_ref, low_ref, own_early_ref, own_lag_ref, series_in_ref, series_ref, slots_ref
):
    group = iota((PLANE, LANES), 1) // OWN
    placed = {}
    for part in range(2):
        sums = got_ref[pl.ds(CAP // 2 + part, OWNERS, stride=ROWS), :] * (1.0 / 8192.0)
        for plane in range(PLANE):
            start = SLOT_PLACE[plane * PLANE]
            value = sums[start:start + PLANE]
            value = value + pltpu.roll(value, 4, 0)
            value = value + pltpu.roll(value, 2, 0)
            for j in range(4):
                turn = (OWN * (plane - j)) % LANES
                moved = pltpu.roll(value, turn, 1) if turn else value
                key = part, j, plane // 4
                placed[key] = jnp.where(group == plane % 4, moved, placed[key]) if key in placed else moved
    group = iota((PLANE, LANES), 1) // SPAN
    sums = got_ref[pl.ds(CAP // 2 + 2, OWNERS, stride=ROWS), :] * (1.0 / 8192.0)
    for plane in range(PLANE):
        start = SLOT_PLACE[plane * PLANE]
        value = sums[start:start + PLANE]
        value = value + pltpu.roll(value, 4, 0)
        value = value + pltpu.roll(value, 2, 0)
        target = (plane - 1) % PLANE
        spot = (target % 4) * 4 + 3
        for row in range(SPAN):
            turn = SPAN * (spot - row) % LANES
            moved = pltpu.roll(value, turn, 1) if turn else value
            key = row // 4, row % 4, target // 4
            placed[key] = placed[key] + jnp.where(group == spot, moved, 0.0)
    rows = [
        jnp.concatenate([placed[part, j, 0], placed[part, j, 1]], axis=1)[core:core + 1]
        for core in range(2) for part in range(2) for j in range(4)
    ]
    total = jnp.concatenate(rows, axis=0)
    high, low = halves(total)
    lag_of = own_lag_ref[:, 0:1]
    shift = [jnp.zeros((1, DATES), F32) for _ in range(2)]
    found = [jnp.zeros((CAP, DATES), F32) for _ in range(2)]
    for lag in range(SPAN):
        rows = slice(lag * DATES, (lag + 1) * DATES)
        part = (
            dot_nt(high, high_ref[:, rows])
            + dot_nt(low, high_ref[:, rows])
            + dot_nt(high, low_ref[:, rows])
        )
        for kind in range(2):
            row = 2 * lag + kind
            shift[kind] = shift[kind] + part[row:row + 1]
            found[kind] = jnp.where(lag_of == float(lag + 1), total[row:row + 1], found[kind])
    means = []
    for kind in range(2):
        rows = slice(kind * LOOKS, (kind + 1) * LOOKS)
        series_ref[rows, :] = series_in_ref[rows, :] - shift[kind]
        means.append(jnp.sum(found[kind] * own_early_ref[...], axis=1, keepdims=True))
    chunk = iota((CAP // 2, LANES), 1) // LOOKS
    for block in range(OWNERS // 4):
        starts = [SLOT_PLACE[4 * block + j] * ROWS for j in range(4)]
        parts = [got_ref[start:start + CAP // 2, :] for start in starts]
        for t in range(4):
            side, kind = t // 2, t % 2
            result = None
            for j in range(4):
                turn = (LOOKS * (j - t)) % LANES
                moved = pltpu.roll(parts[j], turn, 1) if turn else parts[j]
                result = moved if result is None else jnp.where(chunk == j, moved, result)
            rows = slice(side * CAP // 2, (side + 1) * CAP // 2)
            first = (side * CAP + kind) * (OWNERS // 4) + block
            slots_ref[pl.ds(first, CAP // 2, stride=OWNERS // 2), :] = result - means[kind][rows]


def vmem(number):
    return [pl.BlockSpec(memory_space=pltpu.VMEM)] * number


def params(limit=VMEM_LIMIT):
    return pltpu.CompilerParams(vmem_limit_bytes=limit)


def cost(flops, size):
    return pl.CostEstimate(flops=flops, bytes_accessed=size, transcendentals=0)


def along(value, axis_groups):
    return lax.all_to_all(
        value, "acq", split_axis=0, concat_axis=0, tiled=True, axis_index_groups=axis_groups
    )


def exchange_sum(value):
    for axis, steps in (("acq", (1,)), ("strip", (1, 2, 3))):
        size = lax.axis_size(axis)
        moved = [
            lax.ppermute(value, axis, [(i, i ^ step) for i in range(size)]) for step in steps
        ]
        for part in moved:
            value = value + part
    return value


SHAPE = jax.ShapeDtypeStruct
SCALAR = [pl.BlockSpec(memory_space=pltpu.SMEM)]


def pack(slc_stack):
    batch = 2 * PLANE
    return pl.pallas_call(
        pack_kernel,
        out_shape=SHAPE((PLANE, PLANE, LANES, LANES), BF16),
        in_specs=[pl.BlockSpec(memory_space=pl.ANY)],
        out_specs=pl.BlockSpec(memory_space=pl.ANY),
        scratch_shapes=[
            pltpu.VMEM((8, OWNERS, UPPER * LANES), BF16),
            pltpu.VMEM((2, batch * (LANES + 4), LANES), F32),
            pltpu.VMEM((PLANE, PLANE, LANES, LANES), BF16),
            pltpu.SemaphoreType.DMA((OWNERS // batch,)),
            pltpu.SemaphoreType.DMA((OWNERS // batch,)),
        ],
        compiler_params=params(WIDE_LIMIT),
        name="pack",
    )(slc_stack.reshape(8, OWNERS, UPPER * LANES))


def slot_order(mine, date_pairs, pair_owner, pseudo_inverse):
    return pl.pallas_call(
        slot_kernel,
        out_shape=(
            SHAPE((16, SLOTS), F32),
            SHAPE((CAP, DATES), F32),
            SHAPE((CAP, LANES), F32),
            SHAPE((DATES, ENTRIES), BF16),
            SHAPE((DATES, ENTRIES), BF16),
            SHAPE((8 * LANES, TABLE), BF16),
        ),
        in_specs=SCALAR + vmem(3),
        out_specs=tuple(vmem(6)),
        compiler_params=params(),
        name="slot_order",
        cost_estimate=cost(4_000_000_000, 8_000_000),
    )(mine, date_pairs.T, pair_owner.T, pseudo_inverse)


def inner_coherence(cells, table):
    return pl.pallas_call(
        inner_kernel,
        out_shape=(
            SHAPE((PLANE, SPAN // 2 * INNER, LANES), F32),
            SHAPE((2 * SPAN, LANES), F32),
            SHAPE(table.shape, BF16),
        ),
        in_specs=vmem(2),
        out_specs=tuple(vmem(3)),
        scratch_shapes=[
            pltpu.VMEM((4 * TOGETHER, OWN * 8, LANES), F32),
            pltpu.VMEM((PLANE * OWN, 8 * LANES), F32),
            pltpu.VMEM((PLANE * OWN + 8, LANES), F32),
        ],
        compiler_params=params(),
        name="coherence",
        cost_estimate=cost(4_000_000_000, 8_000_000),
    )(cells, table)


def edge_coherence(last, after, before, first, table, inner, inner_sums):
    return pl.pallas_call(
        edge_kernel,
        out_shape=(
            SHAPE((PLANE, SPAN // 2 * OWN, LANES), F32),
            SHAPE((4 * SPAN, LANES), F32),
        ),
        in_specs=vmem(7),
        out_specs=tuple(vmem(2)),
        scratch_shapes=[
            pltpu.VMEM((4 * TOGETHER, 2 * SPAN * 8, LANES), F32),
            pltpu.VMEM((PLANE * 2 * SPAN, 8 * LANES), F32),
            pltpu.VMEM((PLANE * 2 * SPAN + 8, LANES), F32),
        ],
        compiler_params=params(),
        name="edge",
        cost_estimate=cost(2_000_000_000, 4_000_000),
    )(last, after, before, first, table, inner, inner_sums)


def select(mine, coherence, code, sums):
    return pl.pallas_call(
        select_kernel,
        out_shape=SHAPE((OWNERS * ROWS, LANES), F32),
        in_specs=SCALAR + vmem(3),
        out_specs=vmem(1)[0],
        compiler_params=params(),
        name="select",
        cost_estimate=cost(2_000_000_000, 4_000_000),
    )(mine, coherence, code, sums)


def invert(mine, coherence, high, low):
    return pl.pallas_call(
        series_kernel,
        out_shape=SHAPE((2 * LOOKS, DATES), F32),
        in_specs=SCALAR + vmem(3),
        out_specs=vmem(1)[0],
        compiler_params=params(WIDE_LIMIT),
        name="series",
        cost_estimate=cost(1_000_000_000, 3_000_000),
    )(mine, coherence, high, low)


def output(got, high, low, own_early, own_lag, series):
    return pl.pallas_call(
        output_kernel,
        out_shape=(SHAPE((2 * LOOKS, DATES), F32), SHAPE((CAP * 2 * UPPER, LANES), F32)),
        in_specs=vmem(6),
        out_specs=tuple(vmem(2)),
        compiler_params=params(),
        name="referenced",
    )(got, high, low, own_early, own_lag, series)


def on_device(slc_stack, date_pairs, pair_owner, pseudo_inverse):
    size = lax.axis_size("acq")
    planes = [[start + w for w in PLANE_ORDER] for start in range(0, size, PLANE)]
    pillars = [[start + PLANE * z for z in PILLAR_ORDER] for start in range(PLANE)]
    mine = lax.axis_index("acq").astype(jnp.int32).reshape(1)
    cells = along(pack(slc_stack), planes)
    ordered = slot_order(mine, date_pairs, pair_owner, pseudo_inverse)
    cells, ordered = lax.optimization_barrier((cells, ordered))
    code, own_early, own_lag, high, low, table = ordered
    first, last = (
        [cells[PLANE_PLACE[w]:PLANE:PLANE // 2, half:half + HALF] for half in (0, HALF)]
        for w in (0, PLANE - 2)
    )
    after = lax.ppermute(first[0], "acq", [(i, (i - PLANE) % size) for i in range(size)])
    before = lax.ppermute(last[1], "acq", [(i, (i + PLANE) % size) for i in range(size)])
    inner, sums, table = inner_coherence(cells, table)
    parts, sums = edge_coherence(last[0], after, before, first[1], table, inner, sums)
    coherence = along(parts, pillars)
    packed = select(mine, coherence, code, exchange_sum(sums))
    everyone = [[PLANE * z + w for z in SLOT_ORDER for w in range(PLANE)]]
    got = along(packed.reshape(OWNERS, 1, ROWS * LANES), everyone).reshape(OWNERS * ROWS, LANES)
    series = invert(mine, coherence, high, low)
    series, slots = output(got, high, low, own_early, own_lag, series)
    return (
        series.reshape(1, 1, 2, LOOKS, DATES),
        slots.reshape(CAP, 2, 1, OWNERS * LOOKS),
    )


def solution(mesh):
    placed = (P("acq", None, "strip", None, None), P(), P(), P())
    return jax.shard_map(
        on_device,
        mesh=mesh,
        in_specs=placed,
        out_specs=(P("strip", "acq", None, None, None), P("acq", None, "strip", None)),
        check_vma=False,
    )
```
